256 devices in a mesh: lx: 16 (over y_hi, z), ly: 16 (over y_lo, x, core).
Axes of the slice: x: 4, y: 4 (y_hi: 2, y_lo: 2; y = y_hi * 2 + y_lo), z: 8, core: 2. Of those that a mesh axis runs over, the one named last changes fastest.
Arguments:
- site_tensor: bfloat16 [16, 16, 4, 3, 3, 3, 3], P('lx', 'ly'), may hold values from -4 to 4
- phys_charge: int32 [16, 16, 4], P('lx', 'ly'), may hold values from 0 to 2
- virt_charge: int32 [16, 16, 4, 3], P('lx', 'ly'), may hold values from 0 to 2
- env_charge: int32 [16, 16, 2, 128], P('lx', 'ly'), may hold values from 0 to 3
- corner_ul: bfloat16 [16, 16, 128, 128], P('lx', 'ly'), may hold values from -0.5 to 0.5
- corner_ur: bfloat16 [16, 16, 128, 128], P('lx', 'ly'), may hold values from -0.5 to 0.5
- corner_ll: bfloat16 [16, 16, 128, 128], P('lx', 'ly'), may hold values from -0.5 to 0.5
- edge_top: bfloat16 [16, 16, 128, 9, 128], P('lx', 'ly'), may hold values from -0.5 to 0.5
- edge_right: bfloat16 [16, 16, 128, 9, 128], P('lx', 'ly'), may hold values from -0.5 to 0.5
- edge_bottom: bfloat16 [16, 16, 128, 9, 128], P('lx', 'ly'), may hold values from -0.5 to 0.5
- edge_left: bfloat16 [16, 16, 128, 9, 128], P('lx', 'ly'), may hold values from -0.5 to 0.5
- sketch: bfloat16 [16, 16, 4, 1152, 128], P('lx', 'ly'), may hold values from -6 to 6
Outputs:
- left_upper_corner: bfloat16 [16, 16, 128, 128], P('lx', 'ly')
- left_edge_new: bfloat16 [16, 16, 128, 9, 128], P('lx', 'ly')
- left_lower_corner: bfloat16 [16, 16, 128, 128], P('lx', 'ly')
- top_left_corner: bfloat16 [16, 16, 128, 128], P('lx', 'ly')
- top_edge_new: bfloat16 [16, 16, 128, 9, 128], P('lx', 'ly')
- top_right_corner: bfloat16 [16, 16, 128, 128], P('lx', 'ly')
The draws below stay inside these ranges and needn't reach their ends.
All inputs are finite; a program needn't handle non-finite values.
Results may differ from the reference program's by a relative error of at most 0.013.
Values may be sent and summed in bfloat16 or wider, within the bound.
No kernel may reach another device: no remote copies, remote signals or barrier semaphores. Data moves between devices by JAX's collectives and lax.ppermute only.
A program may use at most 128 MiB of HBM per device.

```python
import jax
import jax.numpy as jnp
from jax import lax

CHI = 128
D = 3
PHYS = 4
D2 = 9
CUT = 1152
NX = 16
NY = 16


def touch_ends(result, own_key, least, high):
    spot = [jax.random.randint(jax.random.fold_in(own_key, axis), (), 0, length) for axis, length in enumerate(result.shape)]
    main_axis = result.shape.index(max(result.shape))
    beside = spot[:main_axis] + [(spot[main_axis] + 1) % result.shape[main_axis]] + spot[main_axis + 1:]
    return result.at[tuple(spot)].set(least).at[tuple(beside)].set(high)


def level_of(stream_key, dims, shards, smallest, top_value):
    loudness = 1.0
    for dim, parts in shards:
        steps = jax.random.uniform(jax.random.fold_in(jax.random.fold_in(stream_key, 6), dim), (parts,), jnp.float32, smallest / len(shards), top_value / len(shards))
        loudness = loudness * jnp.repeat(jnp.exp(steps), dims[dim] // parts).reshape((-1,) + (1,) * (len(dims) - 1 - dim))
    return loudness


def bell_draw(stream_key, shape, deviation, most, pieces=(), kind=jnp.bfloat16):
    values = deviation * jax.random.normal(stream_key, shape, jnp.float32)
    if pieces:
        values = values * level_of(stream_key, shape, pieces, -0.22, 0.18)
    return jnp.clip(values, -most, most).astype(kind)


def setup_inputs(seed: int = 0) -> dict:
    splits = jax.random.split(jax.random.key(seed), 13)
    site_tensor = bell_draw(splits[0], (NX, NY, PHYS, D, D, D, D), 0.7, 4.0, ((0, 16), (1, 16)))
    phys_charge = touch_ends(jax.random.randint(splits[1], (NX, NY, PHYS), 0, 3), jax.random.fold_in(splits[1], 1), 0, 2).astype(jnp.int32)
    virt_charge = touch_ends(jax.random.randint(splits[2], (NX, NY, 4, D), 0, 3), jax.random.fold_in(splits[2], 1), 0, 2).astype(jnp.int32)
    env_charge = touch_ends(jax.random.randint(splits[3], (NX, NY, 2, CHI), 0, 4), jax.random.fold_in(splits[3], 1), 0, 3).astype(jnp.int32)
    corner_ul = bell_draw(splits[4], (NX, NY, CHI, CHI), CHI ** -0.5, 0.5, ((0, 16), (1, 16)))
    corner_ur = bell_draw(splits[5], (NX, NY, CHI, CHI), CHI ** -0.5, 0.5, ((0, 16), (1, 16)))
    corner_ll = bell_draw(splits[6], (NX, NY, CHI, CHI), CHI ** -0.5, 0.5, ((0, 16), (1, 16)))
    edge_top = bell_draw(splits[7], (NX, NY, CHI, D2, CHI), CHI ** -0.5, 0.5, ((0, 16), (1, 16)))
    edge_right = bell_draw(splits[8], (NX, NY, CHI, D2, CHI), CHI ** -0.5, 0.5, ((0, 16), (1, 16)))
    edge_bottom = bell_draw(splits[9], (NX, NY, CHI, D2, CHI), CHI ** -0.5, 0.5, ((0, 16), (1, 16)))
    edge_left = bell_draw(splits[10], (NX, NY, CHI, D2, CHI), CHI ** -0.5, 0.5, ((0, 16), (1, 16)))
    sketch = bell_draw(splits[11], (NX, NY, 4, CUT, CHI), 1.0, 6.0, ((0, 16), (1, 16)))
    return dict(site_tensor=site_tensor, phys_charge=phys_charge, virt_charge=virt_charge, env_charge=env_charge, corner_ul=corner_ul, corner_ur=corner_ur, corner_ll=corner_ll, edge_top=edge_top, edge_right=edge_right, edge_bottom=edge_bottom, edge_left=edge_left, sketch=sketch)


def contract(pattern, former, latter):
    return jnp.einsum(pattern, former.astype(jnp.float32), latter.astype(jnp.float32))

def to_half(values):
    return values.astype(jnp.bfloat16)

def unit_rms(values):
    return to_half(values / jnp.sqrt(jnp.mean(values * values) + 1e-06))

def double_layer(site_block, phys_charges, virt_charges):
    charge_sum = phys_charges[:, None, None, None, None] + virt_charges[0][None, :, None, None, None] + virt_charges[1][None, None, :, None, None] - virt_charges[2][None, None, None, :, None] - virt_charges[3][None, None, None, None, :]
    kept_site = jnp.where(charge_sum == 0, site_block, jnp.zeros_like(site_block))
    doubled = contract('slurd,smvpe->lmuvrpde', kept_site, kept_site)
    paired = site_block.shape[1] * site_block.shape[1]
    return to_half(doubled.reshape(paired, paired, paired, paired))

def cut_mask(env_charges, virt_charges, new_charges):
    row_charge = env_charges[:, None, None] + virt_charges[None, :, None] - virt_charges[None, None, :]
    return row_charge.reshape(-1)[:, None] == new_charges[None, :]

def range_basis(sketched):
    gram_matrix = jnp.dot(sketched.T, sketched, precision=lax.Precision.HIGHEST)
    shift_size = 0.01 * jnp.mean(jnp.diagonal(gram_matrix)) + 1e-06
    shifted = gram_matrix + shift_size * jnp.eye(gram_matrix.shape[0], dtype=gram_matrix.dtype)
    factor = jnp.linalg.cholesky(shifted)
    solved = lax.linalg.triangular_solve(factor, sketched, left_side=False, lower=True, transpose_a=True)
    return to_half(solved)

def as_matrix(tensor_in):
    return tensor_in.reshape(tensor_in.shape[0] * tensor_in.shape[1], -1)

def corner_terms(site_block, phys_charges, virt_charges, corner_one, corner_two, corner_low, edge_upper, edge_side_r, edge_lower, edge_side_l, sketches):
    doubled_site = double_layer(site_block, phys_charges, virt_charges)
    corner_edge = to_half(contract('ab,buc->auc', corner_one, edge_upper))
    upper_three = to_half(contract('auc,ale->ucle', corner_edge, edge_side_l))
    upper_left = as_matrix(to_half(contract('ucle,lurd->edcr', upper_three, doubled_site)))
    lower_pair = to_half(contract('ab,bdc->adc', corner_low, edge_lower))
    lower_three = to_half(contract('adc,fla->dcfl', lower_pair, edge_side_l))
    lower_left = as_matrix(to_half(contract('dcfl,lurd->furc', lower_three, doubled_site)))
    right_pair = to_half(contract('ab,bre->are', corner_two, edge_side_r))
    right_three = to_half(contract('are,gua->regu', right_pair, edge_upper))
    upper_right = as_matrix(to_half(contract('regu,lurd->glde', right_three, doubled_site)))
    own_left = jnp.dot(upper_left.astype(jnp.float32), sketches[0].astype(jnp.float32), preferred_element_type=jnp.float32)
    from_lower = jnp.dot(lower_left.astype(jnp.float32), sketches[1].astype(jnp.float32), preferred_element_type=jnp.float32)
    own_top = jnp.dot(upper_left.T.astype(jnp.float32), sketches[2].astype(jnp.float32), preferred_element_type=jnp.float32)
    from_right = jnp.dot(upper_right.astype(jnp.float32), sketches[3].astype(jnp.float32), preferred_element_type=jnp.float32)
    return (own_left, from_lower, own_top, from_right)

def new_tensors(site_block, phys_charges, virt_charges, corner_one, corner_two, corner_low, edge_upper, edge_side_r, edge_lower, edge_side_l, above_basis, left_basis, before_basis, top_basis):
    doubled_site = double_layer(site_block, phys_charges, virt_charges)
    bond_env = corner_one.shape[0]
    paired = doubled_site.shape[0]
    above_proj = above_basis.reshape(bond_env, paired, bond_env)
    own_left = left_basis.reshape(bond_env, paired, bond_env)
    before_proj = before_basis.reshape(bond_env, paired, bond_env)
    own_top = top_basis.reshape(bond_env, paired, bond_env)
    corner_edge = to_half(contract('ab,buc->auc', corner_one, edge_upper))
    lower_pair = to_half(contract('ab,bdc->adc', corner_low, edge_lower))
    right_pair = to_half(contract('ab,bre->are', corner_two, edge_side_r))
    corner_side = to_half(contract('ab,ale->ble', corner_one, edge_side_l))
    left_upper_corner = unit_rms(contract('auk,auc->kc', above_proj, corner_edge))
    side_one = to_half(contract('auk,ale->kule', above_proj, edge_side_l))
    side_two = to_half(contract('kule,lurd->kerd', side_one, doubled_site))
    left_edge_new = unit_rms(contract('kerd,edm->krm', side_two, own_left))
    left_lower_corner = unit_rms(contract('adm,adc->mc', own_left, lower_pair))
    top_left_corner = unit_rms(contract('ble,blk->ek', corner_side, before_proj))
    top_one = to_half(contract('blk,buc->kluc', before_proj, edge_upper))
    top_two = to_half(contract('kluc,lurd->kcrd', top_one, doubled_site))
    top_edge_new = unit_rms(contract('kcrd,crm->kdm', top_two, own_top))
    top_right_corner = unit_rms(contract('arm,are->me', own_top, right_pair))
    return (left_upper_corner, left_edge_new, left_lower_corner, top_left_corner, top_edge_new, top_right_corner)

def flatten_sites(array_in):
    return array_in.reshape((NX * NY,) + array_in.shape[2:])

def unflatten_sites(array_in):
    return array_in.reshape((NX, NY) + array_in.shape[1:])

def reference(site_tensor, phys_charge, virt_charge, env_charge, corner_ul, corner_ur, corner_ll, edge_top, edge_right, edge_bottom, edge_left, sketch):
    inputs = (flatten_sites(site_tensor), flatten_sites(phys_charge), flatten_sites(virt_charge), flatten_sites(corner_ul), flatten_sites(corner_ur), flatten_sites(corner_ll), flatten_sites(edge_top), flatten_sites(edge_right), flatten_sites(edge_bottom), flatten_sites(edge_left), flatten_sites(sketch))
    own_left, from_lower, own_top, from_right = lax.map(lambda packed: corner_terms(*packed), inputs)
    own_left = unflatten_sites(own_left)
    from_lower = unflatten_sites(from_lower)
    own_top = unflatten_sites(own_top)
    from_right = unflatten_sites(from_right)
    masker = jax.vmap(jax.vmap(cut_mask))
    solver = jax.vmap(jax.vmap(range_basis))
    left_mask = masker(env_charge[:, :, 0], virt_charge[:, :, 3], env_charge[:, :, 0])
    left_range = jnp.where(left_mask, own_left + jnp.roll(from_lower, -1, axis=1), 0.0)
    left_basis = solver(left_range)
    top_mask = masker(env_charge[:, :, 1], virt_charge[:, :, 2], env_charge[:, :, 1])
    top_range = jnp.where(top_mask, own_top + jnp.roll(from_right, -1, axis=0), 0.0)
    top_basis = solver(top_range)
    second = inputs[:10] + (flatten_sites(jnp.roll(left_basis, 1, axis=1)), flatten_sites(left_basis), flatten_sites(jnp.roll(top_basis, 1, axis=0)), flatten_sites(top_basis))
    results = lax.map(lambda packed: new_tensors(*packed), second)
    return (unflatten_sites(results[0]), unflatten_sites(results[1]), unflatten_sites(results[2]), unflatten_sites(results[3]), unflatten_sites(results[4]), unflatten_sites(results[5]))
```

```python
import functools

import jax
import jax.numpy as jnp
from jax import lax
from jax.experimental import pallas as pl
from jax.experimental.pallas import tpu as pltpu
from jax.sharding import PartitionSpec as P

F32 = jnp.float32
BF16 = jnp.bfloat16
CHI = 128
D2 = 9
PAD = 16
CUT = CHI * D2
TALL = CHI * PAD
LAY = D2 * PAD
GROUP = 16
CHUNKS = CHI // GROUP
ROWS = GROUP * PAD
VMEM = 56 * 1024 * 1024


def dot(a, b):
    return lax.dot_general(a, b, (((1,), (0,)), ((), ())), preferred_element_type=F32)


def dot_nt(a, b):
    return lax.dot_general(a, b, (((1,), (1,)), ((), ())), preferred_element_type=F32)


def dot_tn(a, b):
    return lax.dot_general(a, b, (((0,), (0,)), ((), ())), preferred_element_type=F32)


def exact_tn(a, b):
    return lax.dot_general(
        a, b, (((0,), (0,)), ((), ())), precision=lax.Precision.HIGHEST, preferred_element_type=F32
    )


def exact_nt(a, b):
    return lax.dot_general(
        a, b, (((1,), (1,)), ((), ())), precision=lax.Precision.HIGHEST, preferred_element_type=F32
    )


def slab(ref, p):
    return ref[p * CHI : (p + 1) * CHI, :]


def side_by_side(ref):
    return jnp.concatenate([slab(ref, p) for p in range(D2)], axis=1)


def spread_rows(slab_of, wide):
    wide[...] = jnp.zeros_like(wide)
    for p in range(D2):
        wide[pl.ds(p, CHI, stride=PAD), :] = slab_of(p).astype(F32)
    return wide[...].astype(BF16)


def gathered_row(wide, p):
    return wide[pl.ds(p, CHI, stride=PAD), :]


def chain(left, right, layer, consume):
    for chunk in range(CHUNKS):
        rows = pl.ds(chunk * ROWS, ROWS)
        three = dot(left[rows, :], right[...]).astype(BF16)
        stacked = jnp.concatenate(
            [
                jnp.concatenate(
                    [
                        three[f * PAD : (f + 1) * PAD, q * CHI : (q + 1) * CHI]
                        for q in range(D2)
                    ],
                    axis=0,
                )
                for f in range(GROUP)
            ],
            axis=1,
        )
        mixed = dot(layer[...], stacked).astype(BF16)
        consume(
            chunk,
            jnp.concatenate(
                [
                    jnp.concatenate(
                        [
                            mixed[s * PAD : (s + 1) * PAD, f * CHI : (f + 1) * CHI]
                            for s in range(D2)
                        ],
                        axis=1,
                    )
                    for f in range(GROUP)
                ],
                axis=0,
            ),
        )


def third(n):
    return (n * 11) >> 5


def layer_masks():
    row = lax.broadcasted_iota(jnp.int32, (LAY, 81), 0)
    lane = lax.broadcasted_iota(jnp.int32, (LAY, 81), 1)
    slow, fast = row >> 4, row & 15
    valid = fast < D2
    pairs = ((third(slow), third(fast)), (slow - 3 * third(slow), fast - 3 * third(fast)))
    leg_l = (lane * 19) >> 9
    rest = lane - 27 * leg_l
    leg_u = (rest * 57) >> 9
    rest = rest - 9 * leg_u
    leg_r = (rest * 11) >> 5
    leg_d = rest - 3 * leg_r

    def mask(slow_leg, fast_leg):
        return [
            jnp.where(valid & (slow_leg == a) & (fast_leg == b), 1.0, 0.0).astype(F32)
            for a, b in pairs
        ]

    return mask(leg_r, leg_u), mask(leg_d, leg_l), mask(leg_r, leg_d), mask(leg_u, leg_l)


def kept_rows(site, phys, virt):
    lane = lax.broadcasted_iota(jnp.int32, (4, 81), 1)
    state = lax.broadcasted_iota(jnp.int32, (4, 81), 0)
    leg_l = (lane * 19) >> 9
    rest = lane - 27 * leg_l
    leg_u = (rest * 57) >> 9
    rest = rest - 9 * leg_u
    leg_r = (rest * 11) >> 5
    leg_d = rest - 3 * leg_r
    total = jnp.zeros((4, 81), jnp.int32)
    for s in range(4):
        total = total + jnp.where(state == s, phys[s], 0)
    for i in range(3):
        total = total + jnp.where(leg_l == i, virt[0, i], 0)
        total = total + jnp.where(leg_u == i, virt[1, i], 0)
        total = total - jnp.where(leg_r == i, virt[2, i], 0)
        total = total - jnp.where(leg_d == i, virt[3, i], 0)
    return jnp.where(total == 0, site[...].astype(F32), 0.0)


def build_layers(kept, out_a, out_b, out_c):
    m_ru, m_dl, m_rd, m_ul = layer_masks()

    def build(rows, cols):
        halves = []
        for half in range(2):
            tall = jnp.concatenate([rows[half] * kept[s : s + 1, :] for s in range(4)], axis=0)
            halves.append(dot_nt(tall.astype(BF16), cols[half].astype(BF16)))
        ket_bra = halves[0] * halves[1]
        total = ket_bra[:LAY]
        for s in range(1, 4):
            total = total + ket_bra[s * LAY : (s + 1) * LAY]
        return total.astype(BF16)

    out_a[...] = build(m_dl, m_ru)
    out_b[...] = build(m_ru, m_dl)
    out_c[...] = build(m_rd, m_ul)


def right_kernel(
    phys, virt, site, corner, edge_r, edge_t, sketch, term, lay_a, lay_b, lay_c, pair_out, wide_t, wide
):
    build_layers(kept_rows(site, phys, virt), lay_a, lay_b, lay_c)
    pair_out[...] = dot(corner[...], side_by_side(edge_r)).astype(BF16)
    wide_t[...] = spread_rows(lambda p: slab(edge_t, p), wide)

    def consume(chunk, block):
        wide[pl.ds(chunk * ROWS, ROWS), :] = dot(block, sketch[...])

    chain(wide_t, pair_out, lay_a, consume)
    for p in range(D2):
        term[p * CHI : (p + 1) * CHI, :] = gathered_row(wide, p).astype(term.dtype)


def lower_kernel(corner, edge_b, edge_l, sketch, lay_b, term, pair_out, wide_l, wide):
    pair_out[...] = dot(corner[...], side_by_side(edge_b)).astype(BF16)
    wide_l[...] = spread_rows(lambda p: slab(edge_l, p), wide)

    def consume(chunk, block):
        wide[pl.ds(chunk * ROWS, ROWS), :] = dot(block, sketch[...])

    chain(wide_l, pair_out, lay_b, consume)
    for p in range(D2):
        term[p * CHI : (p + 1) * CHI, :] = gathered_row(wide, p).astype(term.dtype)


def upper_kernel(
    corner, edge_t, edge_l, sketch_l, sketch_t, lay_c,
    own_left, own_top, corner_edge, corner_side,
    left_rows, sketch_cols, sketch_rows, wide, top_sum,
):
    corner_edge[...] = dot(corner[...], side_by_side(edge_t)).astype(BF16)
    corner_side[...] = dot_tn(corner[...], side_by_side(edge_l)).astype(BF16)
    left_rows[...] = spread_rows(lambda p: jnp.transpose(slab(edge_l, p).astype(F32)), wide)
    wide[0:CUT, :] = sketch_l[...].astype(F32)
    for p in range(D2):
        sketch_cols[p * CHI : (p + 1) * CHI, :] = wide[pl.ds(p, CHI, stride=D2), :].astype(BF16)
    wide[0:CUT, :] = sketch_t[...].astype(F32)
    picked = [wide[pl.ds(p, CHI, stride=D2), :] for p in range(D2)]
    sketch_rows[...] = spread_rows(lambda p: picked[p], wide)
    top_sum[...] = jnp.zeros_like(top_sum)

    def consume(chunk, block):
        rows = pl.ds(chunk * ROWS, ROWS)
        wide[rows, :] = dot(block, sketch_cols[...])
        top_sum[...] += dot_tn(sketch_rows[rows, :], block)

    chain(left_rows, corner_edge, lay_c, consume)
    for p in range(D2):
        own_left[p * CHI : (p + 1) * CHI, :] = gathered_row(wide, p)
        own_top[p * CHI : (p + 1) * CHI, :] = jnp.transpose(top_sum[:, p * CHI : (p + 1) * CHI])


BLOCK = 32


def eliminate(grams):
    count = len(grams)
    row = lax.broadcasted_iota(jnp.int32, (CHI, CHI), 0)
    col = lax.broadcasted_iota(jnp.int32, (CHI, CHI), 1)
    eye = jnp.where(row == col, 1.0, 0.0).astype(F32)
    both = [jnp.concatenate([g, eye], axis=1) for g in grams]
    done = [[] for _ in grams]
    in_row = lax.broadcasted_iota(jnp.int32, (BLOCK, 1), 0)
    for start in range(0, CHI, BLOCK):
        panels = [b[:BLOCK] for b in both]
        roots = [jnp.zeros((BLOCK, 1), F32) for _ in grams]
        for j in range(BLOCK):
            for m in range(count):
                panel = panels[m]
                column = panel[:, start + j : start + j + 1]
                pivot = column[j : j + 1, :]
                scale = jnp.where(in_row > j, column * (1.0 / pivot), 0.0)
                roots[m] = jnp.where(in_row == j, lax.rsqrt(pivot), roots[m])
                panels[m] = panel - scale * panel[j : j + 1, :]
        for m in range(count):
            panels[m] = panels[m] * roots[m]
            done[m].append(panels[m][:, CHI:])
            if start + BLOCK < CHI:
                across = panels[m][:, :CHI]
                update = exact_tn(across, panels[m])[start + BLOCK :]
                both[m] = both[m][BLOCK:] - update
    return [jnp.concatenate(d, axis=0) for d in done]


def basis_kernel(virt, env, own_left, below, own_top, beside, left_out, top_out, range_l, range_t):
    row = lax.broadcasted_iota(jnp.int32, (CHI, CHI), 0)
    col = lax.broadcasted_iota(jnp.int32, (CHI, CHI), 1)
    grams = []
    for side, (own, other, ranged, leg) in enumerate(
        ((own_left, below, range_l, 3), (own_top, beside, range_t, 2))
    ):
        across = jnp.broadcast_to(env[side : side + 1, :].astype(F32), (CHI, CHI))
        gap = across - jnp.transpose(across)
        for p in range(D2):
            shift = (virt[leg, p // 3] - virt[leg, p % 3]).astype(F32)
            total = slab(own, p) + slab(other, p).astype(F32)
            ranged[p * CHI : (p + 1) * CHI, :] = jnp.where(gap == shift, total, 0.0)
        gram = exact_tn(ranged[...], ranged[...])
        diagonal = jnp.where(row == col, gram, 0.0)
        mean = jnp.sum(jnp.sum(diagonal, axis=1, keepdims=True), axis=0, keepdims=True) / CHI
        grams.append(gram + jnp.where(row == col, 0.01 * mean + 1e-06, 0.0))
    inverses = eliminate(grams)
    left_out[...] = exact_nt(range_l[...], inverses[0]).astype(BF16)
    top_out[...] = exact_nt(range_t[...], inverses[1]).astype(BF16)


def unit(values):
    square = jnp.sum(jnp.sum(values * values, axis=1, keepdims=True), axis=0, keepdims=True)
    return (values / jnp.sqrt(square / values.size + 1e-06)).astype(BF16)


def slab_rows(wide_ref, p):
    return wide_ref[:, p * CHI : (p + 1) * CHI]


def corner_from(projector, pair):
    tall = jnp.concatenate([slab_rows(pair, p) for p in range(D2)], axis=0)
    return dot_tn(projector[...], tall)


def final_kernel(
    left, top, above, before, wide_l, wide_t, lay_a, lay_b, corner_edge, corner_side, lower_pair, right_pair,
    out_lu, out_le, out_ll, out_tl, out_te, out_tr,
    beside, spread, wide, total,
):
    out_ll[...] = unit(corner_from(left, lower_pair))
    out_tr[...] = unit(corner_from(top, right_pair))
    out_lu[...] = unit(corner_from(above, corner_edge))
    out_tl[...] = unit(jnp.transpose(corner_from(before, corner_side)))
    for own, other, natural, layer, out in (
        (left, above, wide_l, lay_b, out_le),
        (top, before, wide_t, lay_a, out_te),
    ):
        beside[...] = side_by_side(own)
        spread[...] = spread_rows(lambda p: slab(other, p), wide)
        total[...] = jnp.zeros_like(total)

        def consume(chunk, block):
            total[...] += dot_tn(spread[pl.ds(chunk * ROWS, ROWS), :], block)

        chain(natural, beside, layer, consume)
        result = unit(total[...])
        for p in range(D2):
            out[p * CHI : (p + 1) * CHI, :] = result[:, p * CHI : (p + 1) * CHI]


def shape(*dims, dtype=BF16):
    return jax.ShapeDtypeStruct(dims, dtype)


def vmem_in(count):
    return [pl.BlockSpec(memory_space=pltpu.VMEM)] * count


def smem_in(count):
    return [pl.BlockSpec(memory_space=pltpu.SMEM)] * count


def call(body, name, smem, ins, outs, scratch, flops):
    moved = sum(a.size * a.dtype.itemsize for a in ins) + sum(
        o.size * jnp.dtype(o.dtype).itemsize for o in outs
    )
    return pl.pallas_call(
        body,
        name=name,
        out_shape=tuple(outs),
        in_specs=smem_in(len(smem)) + vmem_in(len(ins)),
        out_specs=tuple(vmem_in(len(outs))),
        scratch_shapes=[pltpu.VMEM(s, d) for s, d in scratch],
        compiler_params=pltpu.CompilerParams(vmem_limit_bytes=VMEM),
        cost_estimate=pl.CostEstimate(flops=flops, bytes_accessed=moved, transcendentals=0),
    )(*smem, *ins)


def from_behind(block, axis, distance):
    size = lax.axis_size(axis)
    route = [((i - distance) % size, i) for i in range(size)]
    return lax.ppermute(block, axis, route)


SEND = BF16


def flat(edge):
    return edge.transpose(1, 0, 2).reshape(CUT, CHI)


def shards(
    site_tensor, phys_charge, virt_charge, env_charge, corner_ul, corner_ur, corner_ll,
    edge_top, edge_right, edge_bottom, edge_left, sketch,
):
    site = site_tensor[0, 0].reshape(4, 81)
    phys, virt, env = phys_charge[0, 0], virt_charge[0, 0], env_charge[0, 0]
    ul, ur, ll = corner_ul[0, 0], corner_ur[0, 0], corner_ll[0, 0]
    top, right, bottom, left = (
        flat(e[0, 0]) for e in (edge_top, edge_right, edge_bottom, edge_left)
    )
    sketches = [sketch[0, 0, i] for i in range(4)]
    tall = shape(CUT, CHI)
    broad = shape(CHI, CUT)
    lay = shape(LAY, LAY)
    padded = shape(TALL, CHI)
    wide = ((TALL, CHI), F32)
    work = 1_000_000_000
    from_right, lay_a, lay_b, lay_c, right_pair, wide_t = call(
        right_kernel, "right", [phys, virt], [site, ur, right, top, sketches[3]],
        [shape(CUT, CHI, dtype=SEND), lay, lay, lay, broad, padded], [wide], work,
    )
    beside = from_behind(from_right, "lx", -1)
    from_lower, lower_pair, wide_l = call(
        lower_kernel, "lower", [], [ll, bottom, left, sketches[1], lay_b],
        [shape(CUT, CHI, dtype=SEND), broad, padded], [wide], work,
    )
    below = from_behind(from_lower, "ly", -1)
    own_left, own_top, corner_edge, corner_side = call(
        upper_kernel, "upper", [], [ul, top, left, sketches[0], sketches[2], lay_c],
        [shape(CUT, CHI, dtype=F32), shape(CUT, CHI, dtype=F32), broad, broad],
        [((TALL, CHI), BF16), ((CUT, CHI), BF16), ((TALL, CHI), BF16), wide, ((CHI, CUT), F32)], work,
    )
    left_basis, top_basis = call(
        basis_kernel, "basis", [virt], [env, own_left, below, own_top, beside], [tall, tall],
        [((CUT, CHI), F32), ((CUT, CHI), F32)], work,
    )
    before = from_behind(top_basis, "lx", 1)
    above = from_behind(left_basis, "ly", 1)
    corner = shape(CHI, CHI)
    lu, le, lo, tl, te, tr = call(
        final_kernel, "final", [],
        [left_basis, top_basis, above, before, wide_l, wide_t, lay_a, lay_b,
         corner_edge, corner_side, lower_pair, right_pair],
        [corner, tall, corner, corner, tall, corner],
        [((CHI, CUT), BF16), ((TALL, CHI), BF16), wide, ((CHI, CUT), F32)], work,
    )
    lift = lambda a: a[None, None]
    edge = lambda a: a.reshape(D2, CHI, CHI).transpose(1, 0, 2)[None, None]
    return lift(lu), edge(le), lift(lo), lift(tl), edge(te), lift(tr)


def solution(mesh):
    split = lambda rest: P("lx", "ly", *([None] * rest))
    in_specs = tuple(split(rest) for rest in (5, 1, 2, 2, 2, 2, 2, 3, 3, 3, 3, 3))
    out_specs = tuple(split(rest) for rest in (2, 3, 2, 2, 3, 2))
    return jax.shard_map(shards, mesh=mesh, in_specs=in_specs, out_specs=out_specs, check_vma=False)
```

```python
import functools

import jax
import jax.numpy as jnp
from jax import lax
from jax.experimental import pallas as pl
from jax.experimental.pallas import tpu as pltpu
from jax.sharding import PartitionSpec as P

F32 = jnp.float32
BF16 = jnp.bfloat16
CHI = 128
D2 = 9
CUT = CHI * D2
TALL = CHI * 8
LAY = 96
GROUP = 32
CHUNKS = CHI // GROUP
ROWS = GROUP * 8
VMEM = 24 * 1024 * 1024


def dot(a, b):
    return lax.dot_general(a, b, (((1,), (0,)), ((), ())), preferred_element_type=F32)


def dot_nt(a, b):
    return lax.dot_general(a, b, (((1,), (1,)), ((), ())), preferred_element_type=F32)


def dot_tn(a, b):
    return lax.dot_general(a, b, (((0,), (0,)), ((), ())), preferred_element_type=F32)


def exact_tn(a, b):
    return lax.dot_general(
        a, b, (((0,), (0,)), ((), ())), precision=lax.Precision.HIGHEST, preferred_element_type=F32
    )


def exact_nt(a, b):
    return lax.dot_general(
        a, b, (((1,), (1,)), ((), ())), precision=lax.Precision.HIGHEST, preferred_element_type=F32
    )


def slab(ref, p):
    return ref[p * CHI : (p + 1) * CHI, :]


def side_by_side(ref):
    return jnp.concatenate([slab(ref, p) for p in range(D2)], axis=1)


def pack_rows(slab_of, wide, out):
    for p in range(8):
        wide[pl.ds(p, CHI, stride=8), :] = slab_of(p).astype(F32)
    out[0:TALL, :] = wide[0:TALL, :].astype(BF16)
    out[TALL:CUT, :] = slab_of(8).astype(BF16)


def packed_slab(wide, p):
    return wide[pl.ds(p, CHI, stride=8), :] if p < 8 else wide[TALL:CUT, :]


def chain(left, right, layer, thin, consume):
    thin[...] = jnp.zeros_like(thin)
    last = dot(left[TALL:CUT, :], right[...])
    for q in range(D2):
        thin[pl.ds(q, CHI, stride=16), :] = last[:, q * CHI : (q + 1) * CHI]
    blank = jnp.zeros((8, CHI), F32)
    for chunk in range(CHUNKS):
        rows = slice(chunk * ROWS, (chunk + 1) * ROWS)
        three = dot(left[rows, :], right[...])
        stacks = []
        for f in range(GROUP):
            here = (chunk * GROUP + f) * 16
            parts = [three[f * 8 : f * 8 + 8, q * CHI : (q + 1) * CHI] for q in range(D2)]
            stack = jnp.concatenate(parts + [thin[here : here + 16, :], blank], axis=0)
            stacks.append(stack.astype(BF16))
        mixed = dot(layer[...], jnp.concatenate(stacks, axis=1))
        tall = []
        for f in range(GROUP):
            here = (chunk * GROUP + f) * 16
            lanes = slice(f * CHI, (f + 1) * CHI)
            thin[here : here + 16, :] = mixed[72:88, lanes]
            tall.append(
                jnp.concatenate([mixed[s * 8 : s * 8 + 8, lanes] for s in range(D2)], axis=1)
            )
        consume(rows, jnp.concatenate(tall, axis=0).astype(BF16))
    rest = [thin[pl.ds(s, CHI, stride=16), :].astype(BF16) for s in range(D2)]
    consume(slice(TALL, CUT), jnp.concatenate(rest, axis=1))


def third(n):
    return (n * 11) >> 5


def layer_masks():
    row = lax.broadcasted_iota(jnp.int32, (LAY, 81), 0)
    lane = lax.broadcasted_iota(jnp.int32, (LAY, 81), 1)
    late = row >= 72
    slow = jnp.where(late, row - 72, row >> 3)
    fast = jnp.where(late, 8, row & 7)
    valid = row < 81
    pairs = ((third(slow), third(fast)), (slow - 3 * third(slow), fast - 3 * third(fast)))
    leg_l = (lane * 19) >> 9
    rest = lane - 27 * leg_l
    leg_u = (rest * 57) >> 9
    rest = rest - 9 * leg_u
    leg_r = (rest * 11) >> 5
    leg_d = rest - 3 * leg_r

    def mask(slow_leg, fast_leg):
        return [
            jnp.where(valid & (slow_leg == a) & (fast_leg == b), 1.0, 0.0).astype(F32)
            for a, b in pairs
        ]

    return mask(leg_r, leg_u), mask(leg_d, leg_l), mask(leg_r, leg_d), mask(leg_u, leg_l)


def kept_rows(site, phys, virt):
    lane = lax.broadcasted_iota(jnp.int32, (4, 81), 1)
    state = lax.broadcasted_iota(jnp.int32, (4, 81), 0)
    leg_l = (lane * 19) >> 9
    rest = lane - 27 * leg_l
    leg_u = (rest * 57) >> 9
    rest = rest - 9 * leg_u
    leg_r = (rest * 11) >> 5
    leg_d = rest - 3 * leg_r
    total = jnp.zeros((4, 81), jnp.int32)
    for s in range(4):
        total = total + jnp.where(state == s, phys[s], 0)
    for i in range(3):
        total = total + jnp.where(leg_l == i, virt[i, 0, 0], 0)
        total = total + jnp.where(leg_u == i, virt[i, 0, 1], 0)
        total = total - jnp.where(leg_r == i, virt[i, 0, 2], 0)
        total = total - jnp.where(leg_d == i, virt[i, 0, 3], 0)
    return jnp.where(total == 0, site[...].astype(F32), 0.0)


def build_layers(kept, out_a, out_b, out_c):
    m_ru, m_dl, m_rd, m_ul = layer_masks()

    def build(rows, cols):
        halves = []
        for half in range(2):
            tall = jnp.concatenate([rows[half] * kept[s : s + 1, :] for s in range(4)], axis=0)
            halves.append(dot_nt(tall.astype(BF16), cols[half].astype(BF16)))
        ket_bra = halves[0] * halves[1]
        total = ket_bra[:LAY]
        for s in range(1, 4):
            total = total + ket_bra[s * LAY : (s + 1) * LAY]
        return total.astype(BF16)

    out_a[...] = build(m_dl, m_ru)
    out_b[...] = build(m_ru, m_dl)
    out_c[...] = build(m_rd, m_ul)


def unpack_term(wide, term):
    for p in range(D2):
        term[p * CHI : (p + 1) * CHI, :] = packed_slab(wide, p).astype(term.dtype)


def right_kernel(
    phys, virt, site, corner, edge_r, edge_t, sketches,
    term, lay_a, lay_b, lay_c, pair_out, rows_t,
    wide, thin, sketch, arrived,
):
    coming = fetch(sketches, 3, sketch, arrived)
    build_layers(kept_rows(site, phys, virt), lay_a, lay_b, lay_c)
    pair_out[...] = dot(corner[...], side_by_side(edge_r)).astype(BF16)
    pack_rows(lambda p: slab(edge_t, p), wide, rows_t)
    coming.wait()

    def consume(rows, block):
        wide[rows, :] = dot(block, sketch[...])

    chain(rows_t, pair_out, lay_a, thin, consume)
    unpack_term(wide, term)


def lower_kernel(
    corner, edge_b, edge_l, lay_b, sketches,
    term, pair_out, rows_l,
    wide, thin, sketch, arrived,
):
    coming = fetch(sketches, 1, sketch, arrived)
    pair_out[...] = dot(corner[...], side_by_side(edge_b)).astype(BF16)
    pack_rows(lambda p: slab(edge_l, p), wide, rows_l)
    coming.wait()

    def consume(rows, block):
        wide[rows, :] = dot(block, sketch[...])

    chain(rows_l, pair_out, lay_b, thin, consume)
    unpack_term(wide, term)


def upper_kernel(
    corner, edge_t, edge_l, lay_c, sketches,
    own_left, own_top, corner_edge, corner_side,
    left_rows, sketch_cols, sketch_rows, wide, thin, top_sum,
    sketch_l, sketch_t, arrived_l, arrived_t,
):
    coming_l = fetch(sketches, 0, sketch_l, arrived_l)
    coming_t = fetch(sketches, 2, sketch_t, arrived_t)
    corner_edge[...] = dot(corner[...], side_by_side(edge_t)).astype(BF16)
    corner_side[...] = dot_tn(corner[...], side_by_side(edge_l)).astype(BF16)
    pack_rows(lambda p: jnp.transpose(slab(edge_l, p).astype(F32)), wide, left_rows)
    coming_l.wait()
    wide[...] = sketch_l[...].astype(F32)
    for p in range(D2):
        sketch_cols[p * CHI : (p + 1) * CHI, :] = wide[pl.ds(p, CHI, stride=D2), :].astype(BF16)
    coming_t.wait()
    wide[...] = sketch_t[...].astype(F32)
    picked = [wide[pl.ds(p, CHI, stride=D2), :] for p in range(D2)]
    pack_rows(lambda p: picked[p], wide, sketch_rows)
    top_sum[...] = jnp.zeros_like(top_sum)

    def consume(rows, block):
        wide[rows, :] = dot(block, sketch_cols[...])
        top_sum[...] += dot_tn(sketch_rows[rows, :], block)

    chain(left_rows, corner_edge, lay_c, thin, consume)
    unpack_term(wide, own_left)
    for p in range(D2):
        own_top[p * CHI : (p + 1) * CHI, :] = jnp.transpose(top_sum[:, p * CHI : (p + 1) * CHI])


BLOCK = 32


def reciprocal(x):
    r = pl.reciprocal(x, approx=True)
    r = r * (2.0 - x * r)
    return r * (2.0 - x * r)


def spread(rows, p):
    return jnp.broadcast_to(rows[p : p + 1, :], (8, CHI))


def eliminate(grams):
    count = len(grams)
    sub = lax.broadcasted_iota(jnp.int32, (8, CHI), 0)
    lane = lax.broadcasted_iota(jnp.int32, (8, CHI), 1)
    groups = CHI // 8
    fact = [[g[8 * i : 8 * i + 8, :] for i in range(groups)] for g in grams]
    inv = [
        [jnp.where(lane == sub + 8 * i, 1.0, 0.0).astype(F32) for i in range(groups)] for _ in grams
    ]
    for start in range(0, groups, BLOCK // 8):
        end = start + BLOCK // 8
        for b in range(start, end):
            cols = [
                [
                    [
                        jnp.broadcast_to(fact[m][g][:, 8 * b + j : 8 * b + j + 1], (8, CHI))
                        for j in range(8)
                    ]
                    for g in range(b, end)
                ]
                for m in range(count)
            ]
            pivots = [jnp.zeros((8, CHI), F32) for _ in grams]
            for p in range(0, 8, 2):
                q = p + 1
                for m in range(count):
                    head = cols[m][0]
                    one, off, two = spread(head[p], p), spread(head[q], p), spread(head[q], q)
                    det = one * two - off * off
                    over_one, over_det = reciprocal(one), reciprocal(det)
                    lead = off * over_one
                    pivots[m] = jnp.where(
                        sub == p, one, jnp.where(sub == q, det * over_one, pivots[m])
                    )
                    later = range(q + 1, 8)
                    row_p = [spread(head[j], p) for j in later]
                    row_q = [spread(head[j], q) for j in later]
                    fact_p, fact_q = spread(fact[m][b], p), spread(fact[m][b], q)
                    inv_p, inv_q = spread(inv[m][b], p), spread(inv[m][b], q)
                    one_d, off_d, two_d = one * over_det, off * over_det, two * over_det
                    for g in range(b, end):
                        own = cols[m][g - b]
                        by_p = own[p] * two_d - own[q] * off_d
                        by_q = own[q] * one_d - own[p] * off_d
                        if g == b:
                            by_p = jnp.where(sub > q, by_p, jnp.where(sub == q, lead, 0.0))
                            by_q = jnp.where(sub > q, by_q, 0.0)
                        for n, j in enumerate(later):
                            own[j] = own[j] - by_p * row_p[n] - by_q * row_q[n]
                        fact[m][g] = fact[m][g] - by_p * fact_p - by_q * fact_q
                        inv[m][g] = inv[m][g] - by_p * inv_p - by_q * inv_q
            for m in range(count):
                root = lax.rsqrt(pivots[m])
                fact[m][b] = fact[m][b] * root
                inv[m][b] = inv[m][b] * root
        if end < groups:
            for m in range(count):
                upper = jnp.concatenate(fact[m][start:end], axis=0)
                both = jnp.concatenate([upper, jnp.concatenate(inv[m][start:end], axis=0)], axis=1)
                update = exact_tn(upper, both)
                for g in range(end, groups):
                    fact[m][g] = fact[m][g] - update[8 * g : 8 * g + 8, :CHI]
                    inv[m][g] = inv[m][g] - update[8 * g : 8 * g + 8, CHI:]
    return [jnp.concatenate(i, axis=0) for i in inv]


def basis_kernel(virt, env, own_left, below, own_top, beside, left_out, top_out, range_l, range_t):
    row = lax.broadcasted_iota(jnp.int32, (CHI, CHI), 0)
    col = lax.broadcasted_iota(jnp.int32, (CHI, CHI), 1)
    grams = []
    for side, (own, other, ranged, leg) in enumerate(
        ((own_left, below, range_l, 3), (own_top, beside, range_t, 2))
    ):
        across = jnp.broadcast_to(env[side : side + 1, :].astype(F32), (CHI, CHI))
        gap = across - jnp.transpose(across)
        for p in range(D2):
            shift = (virt[p // 3, 0, leg] - virt[p % 3, 0, leg]).astype(F32)
            total = slab(own, p) + slab(other, p).astype(F32)
            ranged[p * CHI : (p + 1) * CHI, :] = jnp.where(gap == shift, total, 0.0)
        gram = exact_tn(ranged[...], ranged[...])
        diagonal = jnp.where(row == col, gram, 0.0)
        mean = jnp.sum(jnp.sum(diagonal, axis=1, keepdims=True), axis=0, keepdims=True) / CHI
        grams.append(gram + jnp.where(row == col, 0.01 * mean + 1e-06, 0.0))
    inverses = eliminate(grams)
    left_out[...] = exact_nt(range_l[...], inverses[0]).astype(BF16)
    top_out[...] = exact_nt(range_t[...], inverses[1]).astype(BF16)


def unit(values):
    square = jnp.sum(jnp.sum(values * values, axis=1, keepdims=True), axis=0, keepdims=True)
    return (values / jnp.sqrt(square / values.size + 1e-06)).astype(BF16)


def slab_rows(wide_ref, p):
    return wide_ref[:, p * CHI : (p + 1) * CHI]


def corner_from(projector, pair):
    tall = jnp.concatenate([slab_rows(pair, p) for p in range(D2)], axis=0)
    return dot_tn(projector[...], tall)


def own_kernel(
    left, top, rows_l, rows_t, lay_a, lay_b, lower_pair, right_pair,
    out_ll, out_tr, mixed_l, mixed_t,
    beside, thin,
):
    for own, natural, layer, mixed in ((left, rows_l, lay_b, mixed_l), (top, rows_t, lay_a, mixed_t)):
        beside[...] = side_by_side(own)

        def consume(rows, block):
            mixed[rows, :] = block

        chain(natural, beside, layer, thin, consume)
    out_ll[...] = unit(corner_from(left, lower_pair))
    out_tr[...] = unit(corner_from(top, right_pair))


def final_kernel(
    above, before, mixed_l, mixed_t, corner_edge, corner_side,
    out_lu, out_le, out_tl, out_te,
    packed, wide,
):
    for other, mixed, out in ((above, mixed_l, out_le), (before, mixed_t, out_te)):
        pack_rows(lambda p: slab(other, p), wide, packed)
        result = unit(dot_tn(packed[...], mixed[...]))
        for p in range(D2):
            out[p * CHI : (p + 1) * CHI, :] = result[:, p * CHI : (p + 1) * CHI]
    out_lu[...] = unit(corner_from(above, corner_edge))
    out_tl[...] = unit(jnp.transpose(corner_from(before, corner_side)))


def shape(*dims, dtype=BF16):
    return jax.ShapeDtypeStruct(dims, dtype)


def vmem_in(count):
    return [pl.BlockSpec(memory_space=pltpu.VMEM)] * count


def smem_in(count):
    return [pl.BlockSpec(memory_space=pltpu.SMEM)] * count


def fetch(sketches, index, buffer, arrived):
    copy = pltpu.make_async_copy(sketches.at[pl.ds(index * CUT, CUT), :], buffer, arrived)
    copy.start()
    return copy


def call(body, name, smem, ins, outs, scratch, flops, fetches=0):
    moved = sum(a.size * a.dtype.itemsize for a in ins) + sum(
        o.size * jnp.dtype(o.dtype).itemsize for o in outs
    )
    specs = vmem_in(len(ins))
    buffers = [pltpu.VMEM(s, d) for s, d in scratch]
    if fetches:
        specs[-1] = pl.BlockSpec(memory_space=pl.ANY)
        buffers += [pltpu.VMEM((CUT, CHI), BF16)] * fetches + [pltpu.SemaphoreType.DMA] * fetches
    return pl.pallas_call(
        body,
        name=name,
        out_shape=tuple(outs),
        in_specs=smem_in(len(smem)) + specs,
        out_specs=tuple(vmem_in(len(outs))),
        scratch_shapes=buffers,
        compiler_params=pltpu.CompilerParams(vmem_limit_bytes=VMEM),
        cost_estimate=pl.CostEstimate(flops=flops, bytes_accessed=moved, transcendentals=0),
    )(*smem, *ins)


def from_behind(block, axis, distance):
    size = lax.axis_size(axis)
    route = [((i - distance) % size, i) for i in range(size)]
    return lax.ppermute(block, axis, route)


SEND = BF16


def flat(edge):
    return edge.transpose(1, 0, 2).reshape(CUT, CHI)


def shards(
    site_tensor, phys_charge, virt_charge, env_charge, corner_ul, corner_ur, corner_ll,
    edge_top, edge_right, edge_bottom, edge_left, sketch,
):
    site = site_tensor[0, 0].reshape(4, 81)
    phys, env = phys_charge[0, 0], env_charge[0, 0]
    virt = virt_charge[0, 0].T[:, None, :]
    ul, ur, ll = corner_ul[0, 0], corner_ur[0, 0], corner_ll[0, 0]
    top, right, bottom, left = (
        flat(e[0, 0]) for e in (edge_top, edge_right, edge_bottom, edge_left)
    )
    sketches = sketch[0, 0].reshape(4 * CUT, CHI)
    tall = shape(CUT, CHI)
    broad = shape(CHI, CUT)
    lay = shape(LAY, LAY)
    wide = ((CUT, CHI), F32)
    thin = ((CHI * 16, CHI), F32)
    square = shape(CUT, CUT)
    work = 1_000_000_000
    from_right, lay_a, lay_b, lay_c, right_pair, rows_t = call(
        right_kernel, "right", [phys, virt], [site, ur, right, top, sketches],
        [shape(CUT, CHI, dtype=SEND), lay, lay, lay, broad, tall], [wide, thin], work, 1,
    )
    beside = from_behind(from_right, "lx", -1)
    from_lower, lower_pair, rows_l = call(
        lower_kernel, "lower", [], [ll, bottom, left, lay_b, sketches],
        [shape(CUT, CHI, dtype=SEND), broad, tall], [wide, thin], work, 1,
    )
    below = from_behind(from_lower, "ly", -1)
    own_left, own_top, corner_edge, corner_side = call(
        upper_kernel, "upper", [], [ul, top, left, lay_c, sketches],
        [shape(CUT, CHI, dtype=F32), shape(CUT, CHI, dtype=F32), broad, broad],
        [((CUT, CHI), BF16), ((CUT, CHI), BF16), ((CUT, CHI), BF16), wide, thin, ((CHI, CUT), F32)],
        work, 2,
    )
    left_basis, top_basis = call(
        basis_kernel, "basis", [virt], [env, own_left, below, own_top, beside], [tall, tall],
        [((CUT, CHI), F32), ((CUT, CHI), F32)], work,
    )
    before = from_behind(top_basis, "lx", 1)
    above = from_behind(left_basis, "ly", 1)
    corner = shape(CHI, CHI)
    lo, tr, mixed_l, mixed_t = call(
        own_kernel, "own", [],
        [left_basis, top_basis, rows_l, rows_t, lay_a, lay_b, lower_pair, right_pair],
        [corner, corner, square, square], [((CHI, CUT), BF16), thin], work,
    )
    lu, le, tl, te = call(
        final_kernel, "final", [], [above, before, mixed_l, mixed_t, corner_edge, corner_side],
        [corner, tall, corner, tall], [((CUT, CHI), BF16), wide], work,
    )
    lift = lambda a: a[None, None]
    edge = lambda a: a.reshape(D2, CHI, CHI).transpose(1, 0, 2)[None, None]
    return lift(lu), edge(le), lift(lo), lift(tl), edge(te), lift(tr)


def solution(mesh):
    split = lambda rest: P("lx", "ly", *([None] * rest))
    in_specs = tuple(split(rest) for rest in (5, 1, 2, 2, 2, 2, 2, 3, 3, 3, 3, 3))
    out_specs = tuple(split(rest) for rest in (2, 3, 2, 2, 3, 2))
    return jax.shard_map(shards, mesh=mesh, in_specs=in_specs, out_specs=out_specs, check_vma=False)
```

```python
import functools

import jax
import jax.numpy as jnp
from jax import lax
from jax.experimental import pallas as pl
from jax.experimental.pallas import tpu as pltpu
from jax.sharding import PartitionSpec as P

F32 = jnp.float32
BF16 = jnp.bfloat16
CHI = 128
D2 = 9
CUT = CHI * D2
TALL = CHI * 8
LAY = 96
GROUP = 32
CHUNKS = CHI // GROUP
ROWS = GROUP * 8
VMEM = 24 * 1024 * 1024
WORK = (10_000_000,) * 5


def dot(a, b):
    return lax.dot_general(a, b, (((1,), (0,)), ((), ())), preferred_element_type=F32)


def dot_nt(a, b):
    return lax.dot_general(a, b, (((1,), (1,)), ((), ())), preferred_element_type=F32)


def dot_tn(a, b):
    return lax.dot_general(a, b, (((0,), (0,)), ((), ())), preferred_element_type=F32)


def exact_tn(a, b):
    return lax.dot_general(
        a, b, (((0,), (0,)), ((), ())), precision=lax.Precision.HIGHEST, preferred_element_type=F32
    )


def exact_nt(a, b):
    return lax.dot_general(
        a, b, (((1,), (1,)), ((), ())), precision=lax.Precision.HIGHEST, preferred_element_type=F32
    )


def slab(ref, p):
    return ref[p * CHI : (p + 1) * CHI, :]


def side_by_side(ref):
    return jnp.concatenate([slab(ref, p) for p in range(D2)], axis=1)


def pack_rows(slab_of, wide, out):
    for p in range(8):
        wide[pl.ds(p, CHI, stride=8), :] = slab_of(p).astype(F32)
    out[0:TALL, :] = wide[0:TALL, :].astype(BF16)
    out[TALL:CUT, :] = slab_of(8).astype(BF16)


def packed_slab(wide, p):
    return wide[pl.ds(p, CHI, stride=8), :] if p < 8 else wide[TALL:CUT, :]


def chain(left, right, layer, thin, consume):
    thin[...] = jnp.zeros_like(thin)
    last = dot(left[TALL:CUT, :], right[...])
    for q in range(D2):
        thin[pl.ds(q, CHI, stride=16), :] = last[:, q * CHI : (q + 1) * CHI]
    blank = jnp.zeros((8, CHI), F32)
    for chunk in range(CHUNKS):
        rows = slice(chunk * ROWS, (chunk + 1) * ROWS)
        three = dot(left[rows, :], right[...])
        stacks = []
        for f in range(GROUP):
            here = (chunk * GROUP + f) * 16
            parts = [three[f * 8 : f * 8 + 8, q * CHI : (q + 1) * CHI] for q in range(D2)]
            stack = jnp.concatenate(parts + [thin[here : here + 16, :], blank], axis=0)
            stacks.append(stack.astype(BF16))
        mixed = dot(layer[...], jnp.concatenate(stacks, axis=1))
        tall = []
        for f in range(GROUP):
            here = (chunk * GROUP + f) * 16
            lanes = slice(f * CHI, (f + 1) * CHI)
            thin[here : here + 16, :] = mixed[72:88, lanes]
            tall.append(
                jnp.concatenate([mixed[s * 8 : s * 8 + 8, lanes] for s in range(D2)], axis=1)
            )
        consume(rows, jnp.concatenate(tall, axis=0).astype(BF16))
    rest = [thin[pl.ds(s, CHI, stride=16), :].astype(BF16) for s in range(D2)]
    consume(slice(TALL, CUT), jnp.concatenate(rest, axis=1))


def third(n):
    return (n * 11) >> 5


def layer_masks():
    row = lax.broadcasted_iota(jnp.int32, (LAY, 81), 0)
    lane = lax.broadcasted_iota(jnp.int32, (LAY, 81), 1)
    late = row >= 72
    slow = jnp.where(late, row - 72, row >> 3)
    fast = jnp.where(late, 8, row & 7)
    valid = row < 81
    pairs = ((third(slow), third(fast)), (slow - 3 * third(slow), fast - 3 * third(fast)))
    leg_l = (lane * 19) >> 9
    rest = lane - 27 * leg_l
    leg_u = (rest * 57) >> 9
    rest = rest - 9 * leg_u
    leg_r = (rest * 11) >> 5
    leg_d = rest - 3 * leg_r

    def mask(slow_leg, fast_leg):
        return [
            jnp.where(valid & (slow_leg == a) & (fast_leg == b), 1.0, 0.0).astype(F32)
            for a, b in pairs
        ]

    return mask(leg_r, leg_u), mask(leg_d, leg_l), mask(leg_r, leg_d), mask(leg_u, leg_l)


def kept_rows(site, phys, virt, corner):
    lane = lax.broadcasted_iota(jnp.int32, (8, 81), 1)
    state = lax.broadcasted_iota(jnp.int32, (8, 81), 0)
    leg_l = (lane * 19) >> 9
    rest = lane - 27 * leg_l
    leg_u = (rest * 57) >> 9
    rest = rest - 9 * leg_u
    leg_r = (rest * 11) >> 5
    leg_d = rest - 3 * leg_r
    total = jnp.zeros((8, 81), jnp.int32)
    for s in range(4):
        total = total + jnp.where(state == s, phys[0, 0, s], 0)
    for i in range(3):
        total = total + jnp.where(leg_l == i, virt[i, 0, 0], 0)
        total = total + jnp.where(leg_u == i, virt[i, 0, 1], 0)
        total = total - jnp.where(leg_r == i, virt[i, 0, 2], 0)
        total = total - jnp.where(leg_d == i, virt[i, 0, 3], 0)
    corner[...] = jnp.zeros_like(corner)
    for n in range(27):
        corner[8 * n : 8 * n + 4, 0:3] = site[n].astype(F32)
    lane = lax.broadcasted_iota(jnp.int32, (CHI, 81), 1)
    leg = lax.broadcasted_iota(jnp.int32, (CHI, 81), 0)
    place = jnp.where(lane - 3 * ((lane * 683) >> 11) == leg, 1.0, 0.0).astype(BF16)
    wide_site = dot(corner[...].astype(BF16), place)
    block = lax.broadcasted_iota(jnp.int32, (216, 81), 0) >> 3
    lane = lax.broadcasted_iota(jnp.int32, (216, 81), 1)
    wide_site = jnp.where((lane * 683) >> 11 == block, wide_site, 0.0)
    rows = wide_site[0:8]
    for n in range(1, 27):
        rows = rows + wide_site[8 * n : 8 * n + 8]
    return jnp.where(total == 0, rows, 0.0)


def build_layers(kept, out_a, out_b, out_c):
    m_ru, m_dl, m_rd, m_ul = layer_masks()

    def build(rows, cols):
        halves = []
        for half in range(2):
            tall = jnp.concatenate([rows[half] * kept[s : s + 1, :] for s in range(4)], axis=0)
            halves.append(dot_nt(tall.astype(BF16), cols[half].astype(BF16)))
        ket_bra = halves[0] * halves[1]
        total = ket_bra[:LAY]
        for s in range(1, 4):
            total = total + ket_bra[s * LAY : (s + 1) * LAY]
        return total.astype(BF16)

    out_a[...] = build(m_dl, m_ru)
    out_b[...] = build(m_ru, m_dl)
    out_c[...] = build(m_rd, m_ul)


def unpack_term(wide, term, sent):
    for p in range(D2):
        part = packed_slab(wide, p)
        term[p * CHI : (p + 1) * CHI, :] = part
        sent[p * CHI : (p + 1) * CHI, :] = part.astype(BF16)


def add_charges(sent, env, virt, leg):
    sent[CUT : CUT + 16, :] = jnp.concatenate(
        [env]
        + [
            jnp.full((1, CHI), (virt[p // 3, 0, leg] - virt[p % 3, 0, leg]).astype(F32))
            for p in range(D2)
        ]
        + [jnp.zeros((6, CHI), F32)],
        axis=0,
    ).astype(BF16)


def bring(sources, targets, arrived):
    copies = [
        pltpu.make_async_copy(source, target, arrived.at[i])
        for i, (source, target) in enumerate(zip(sources, targets))
    ]
    for copy in copies:
        copy.start()
    return copies


def upper_kernel(
    phys_h, virt_h, site_h, env_h, corner_h, edge_t_h, edge_l_h, sketches,
    own_left, own_top, sent_left, sent_top, corner_edge, corner_side, lay_a, lay_b,
    phys, virt, site, env, corner, edge_t, edge_l, sketch_l, sketch_t, arrived,
    left_rows, sketch_cols, sketch_rows, wide, thin, top_sum, lay_c, small,
):
    first = sketches.at[pl.ds(0, CUT), :]
    third_one = sketches.at[pl.ds(2 * CUT, CUT), :]
    copies = bring(
        (phys_h, virt_h, site_h, env_h, corner_h, edge_t_h, edge_l_h, first, third_one),
        (phys, virt, site, env, corner, edge_t, edge_l, sketch_l, sketch_t),
        arrived,
    )
    for copy in copies[:4]:
        copy.wait()
    build_layers(kept_rows(site, phys, virt, small), lay_a, lay_b, lay_c)
    charges = env[...].astype(F32)
    add_charges(sent_left, charges[0:1], virt, 3)
    add_charges(sent_top, charges[1:2], virt, 2)
    for copy in copies[4:7]:
        copy.wait()
    corner_edge[...] = dot(corner[...], side_by_side(edge_t)).astype(BF16)
    corner_side[...] = dot_tn(corner[...], side_by_side(edge_l)).astype(BF16)
    pack_rows(lambda p: jnp.transpose(slab(edge_l, p).astype(F32)), wide, left_rows)
    copies[7].wait()
    wide[...] = sketch_l[...].astype(F32)
    for p in range(D2):
        sketch_cols[p * CHI : (p + 1) * CHI, :] = wide[pl.ds(p, CHI, stride=D2), :].astype(BF16)
    copies[8].wait()
    wide[...] = sketch_t[...].astype(F32)
    picked = [wide[pl.ds(p, CHI, stride=D2), :] for p in range(D2)]
    pack_rows(lambda p: picked[p], wide, sketch_rows)
    top_sum[...] = jnp.zeros_like(top_sum)

    def consume(rows, block):
        wide[rows, :] = dot(block, sketch_cols[...])
        top_sum[...] += dot_tn(sketch_rows[rows, :], block)

    chain(left_rows, corner_edge, lay_c, thin, consume)
    unpack_term(wide, own_left, sent_left)
    for p in range(D2):
        part = jnp.transpose(top_sum[:, p * CHI : (p + 1) * CHI])
        own_top[p * CHI : (p + 1) * CHI, :] = part
        sent_top[p * CHI : (p + 1) * CHI, :] = part.astype(BF16)


def other_kernel(
    which, layer, corner_h, edge_h, edge_rows_h, sketches,
    term, sent, pair_out, rows_out,
    corner, edge, edge_rows, sketch, arrived, wide, thin,
):
    copies = bring(
        (corner_h, edge_h, edge_rows_h, sketches.at[pl.ds(which * CUT, CUT), :]),
        (corner, edge, edge_rows, sketch),
        arrived,
    )
    for copy in copies[:3]:
        copy.wait()
    pair_out[...] = dot(corner[...], side_by_side(edge)).astype(BF16)
    pack_rows(lambda p: slab(edge_rows, p), wide, rows_out)
    copies[3].wait()

    def consume(rows, block):
        wide[rows, :] = dot(block, sketch[...])

    chain(rows_out, pair_out, layer, thin, consume)
    unpack_term(wide, term, sent)


BLOCK = 32


def reciprocal(x):
    r = pl.reciprocal(x, approx=True)
    r = r * (2.0 - x * r)
    return r * (2.0 - x * r)


def spread(rows, p):
    return jnp.broadcast_to(rows[p : p + 1, :], (8, CHI))


def eliminate(grams):
    count = len(grams)
    sub = lax.broadcasted_iota(jnp.int32, (8, CHI), 0)
    lane = lax.broadcasted_iota(jnp.int32, (8, CHI), 1)
    groups = CHI // 8
    fact = [[g[8 * i : 8 * i + 8, :] for i in range(groups)] for g in grams]
    inv = [
        [jnp.where(lane == sub + 8 * i, 1.0, 0.0).astype(F32) for i in range(groups)] for _ in grams
    ]
    for start in range(0, groups, BLOCK // 8):
        end = start + BLOCK // 8
        for b in range(start, end):
            cols = [
                [
                    [
                        jnp.broadcast_to(fact[m][g][:, 8 * b + j : 8 * b + j + 1], (8, CHI))
                        for j in range(8)
                    ]
                    for g in range(b, end)
                ]
                for m in range(count)
            ]
            pivots = [jnp.zeros((8, CHI), F32) for _ in grams]
            for p in range(0, 8, 2):
                q = p + 1
                for m in range(count):
                    head = cols[m][0]
                    one, off, two = spread(head[p], p), spread(head[q], p), spread(head[q], q)
                    det = one * two - off * off
                    over_one, over_det = reciprocal(one), reciprocal(det)
                    lead = off * over_one
                    pivots[m] = jnp.where(
                        sub == p, one, jnp.where(sub == q, det * over_one, pivots[m])
                    )
                    later = range(q + 1, 8)
                    row_p = [spread(head[j], p) for j in later]
                    row_q = [spread(head[j], q) for j in later]
                    fact_p, fact_q = spread(fact[m][b], p), spread(fact[m][b], q)
                    inv_p, inv_q = spread(inv[m][b], p), spread(inv[m][b], q)
                    one_d, off_d, two_d = one * over_det, off * over_det, two * over_det
                    for g in range(b, end):
                        own = cols[m][g - b]
                        by_p = own[p] * two_d - own[q] * off_d
                        by_q = own[q] * one_d - own[p] * off_d
                        if g == b:
                            by_p = jnp.where(sub > q, by_p, jnp.where(sub == q, lead, 0.0))
                            by_q = jnp.where(sub > q, by_q, 0.0)
                        for n, j in enumerate(later):
                            own[j] = own[j] - by_p * row_p[n] - by_q * row_q[n]
                        fact[m][g] = fact[m][g] - by_p * fact_p - by_q * fact_q
                        inv[m][g] = inv[m][g] - by_p * inv_p - by_q * inv_q
            for m in range(count):
                root = lax.rsqrt(pivots[m])
                fact[m][b] = fact[m][b] * root
                inv[m][b] = inv[m][b] * root
        if end < groups:
            for m in range(count):
                upper = jnp.concatenate(fact[m][start:end], axis=0)
                both = jnp.concatenate([upper, jnp.concatenate(inv[m][start:end], axis=0)], axis=1)
                update = exact_tn(upper, both)
                for g in range(end, groups):
                    fact[m][g] = fact[m][g] - update[8 * g : 8 * g + 8, :CHI]
                    inv[m][g] = inv[m][g] - update[8 * g : 8 * g + 8, CHI:]
    return [jnp.concatenate(i, axis=0) for i in inv]


def halves(values):
    high = values.astype(BF16)
    return high, (values - high.astype(F32)).astype(BF16)


def gram_of(ranged):
    high, low = halves(ranged)
    cross = dot_tn(high, low)
    return dot_tn(high, high) + (cross + jnp.transpose(cross))


def times_inverse(ranged, inverse):
    high, low = halves(ranged)
    inv_high, inv_low = halves(inverse)
    return dot_nt(high, inv_high) + (dot_nt(high, inv_low) + dot_nt(low, inv_high))


def unit(values):
    square = jnp.sum(jnp.sum(values * values, axis=1, keepdims=True), axis=0, keepdims=True)
    return (values / jnp.sqrt(square / values.size + 1e-06)).astype(BF16)


def slab_rows(wide_ref, p):
    return wide_ref[:, p * CHI : (p + 1) * CHI]


def corner_from(projector, pair):
    tall = jnp.concatenate([slab_rows(pair, p) for p in range(D2)], axis=0)
    return dot_tn(projector[...], tall)


def bond_kernel(
    side, leg, virt_h, env_h, own, own_other, near, far, natural, layer, pair_own, pair_far,
    out_own, out_edge, out_far,
    virt, env, arrived, ranged, basis_own, basis_far, beside, packed, wide, thin, total,
):
    copies = bring((virt_h, env_h), (virt, env), arrived)
    for copy in copies:
        copy.wait()
    row = lax.broadcasted_iota(jnp.int32, (CHI, CHI), 0)
    col = lax.broadcasted_iota(jnp.int32, (CHI, CHI), 1)
    grams = []
    for which in range(2):
        if which == 0:
            first, second = own, near
            charges = env[side : side + 1, :].astype(F32)
            shifts = [
                (virt[p // 3, 0, leg] - virt[p % 3, 0, leg]).astype(F32) for p in range(D2)
            ]
        else:
            first, second = own_other, far
            tags = far[CUT : CUT + 16, :].astype(F32)
            charges = tags[0:1]
            shifts = [tags[1 + p : 2 + p] for p in range(D2)]
        across = jnp.broadcast_to(charges, (CHI, CHI))
        gap = across - jnp.transpose(across)
        for p in range(D2):
            sums = slab(first, p) + slab(second, p).astype(F32)
            ranged[which * CUT + p * CHI : which * CUT + (p + 1) * CHI, :] = jnp.where(
                gap == shifts[p], sums, 0.0
            )
        gram = gram_of(ranged[which * CUT : (which + 1) * CUT, :])
        diagonal = jnp.where(row == col, gram, 0.0)
        mean = jnp.sum(jnp.sum(diagonal, axis=1, keepdims=True), axis=0, keepdims=True) / CHI
        grams.append(gram + jnp.where(row == col, 0.01 * mean + 1e-06, 0.0))
    inverses = eliminate(grams)
    basis_own[...] = times_inverse(ranged[0:CUT, :], inverses[0]).astype(BF16)
    basis_far[...] = times_inverse(ranged[CUT : 2 * CUT, :], inverses[1]).astype(BF16)
    beside[...] = side_by_side(basis_own)
    pack_rows(lambda p: slab(basis_far, p), wide, packed)
    total[...] = jnp.zeros_like(total)

    def consume(rows, block):
        total[...] += dot_tn(packed[rows, :], block)

    chain(natural, beside, layer, thin, consume)
    result = unit(total[...])
    for p in range(D2):
        out_edge[p * CHI : (p + 1) * CHI, :] = result[:, p * CHI : (p + 1) * CHI]
    out_own[...] = unit(corner_from(basis_own, pair_own))
    far_corner = corner_from(basis_far, pair_far)
    out_far[...] = unit(jnp.transpose(far_corner) if side else far_corner)


def shape(*dims, dtype=BF16):
    return jax.ShapeDtypeStruct(dims, dtype)


def call(body, name, ins, outs, scratch, flops, far=()):
    moved = sum(a.size * a.dtype.itemsize for a in ins) + sum(
        o.size * jnp.dtype(o.dtype).itemsize for o in outs
    )
    whole = pl.BlockSpec(memory_space=pltpu.VMEM)
    return pl.pallas_call(
        body,
        name=name,
        out_shape=tuple(outs),
        in_specs=[
            pl.BlockSpec(memory_space=pltpu.HBM) if i in far else whole for i in range(len(ins))
        ],
        out_specs=(whole,) * len(outs),
        scratch_shapes=scratch,
        compiler_params=pltpu.CompilerParams(vmem_limit_bytes=VMEM if name != "upper" else 60 * 1024 * 1024),
        cost_estimate=pl.CostEstimate(flops=flops, bytes_accessed=moved, transcendentals=0),
    )(*ins)


def from_behind(block, axis, distance):
    size = lax.axis_size(axis)
    route = [((i - distance) % size, i) for i in range(size)]
    return lax.ppermute(block, axis, route)


def flat(edge):
    return edge.transpose(1, 0, 2).reshape(CUT, CHI)


def shards(
    site_tensor, phys_charge, virt_charge, env_charge, corner_ul, corner_ur, corner_ll,
    edge_top, edge_right, edge_bottom, edge_left, sketch,
):
    site = site_tensor.transpose(0, 1, 3, 4, 5, 2, 6).reshape(27, 4, 3)
    virt = virt_charge.transpose(0, 3, 1, 2).reshape(3, 1, 4)
    env = env_charge[0, 0]
    ul, ur, ll = corner_ul[0, 0], corner_ur[0, 0], corner_ll[0, 0]
    top, right, bottom, left = (
        flat(e[0, 0]) for e in (edge_top, edge_right, edge_bottom, edge_left)
    )
    sketches = sketch[0, 0].reshape(4 * CUT, CHI)
    tall = shape(CUT, CHI)
    tall_wide = shape(CUT, CHI, dtype=F32)
    tagged = shape(CUT + 16, CHI)
    broad = shape(CHI, CUT)
    lay = shape(LAY, LAY)
    corner = shape(CHI, CHI)
    keep = lambda *dims, dtype=BF16: pltpu.VMEM(dims, dtype)
    slabs = keep(CUT, CHI)
    wide = keep(CUT, CHI, dtype=F32)
    thin = keep(CHI * 16, CHI, dtype=F32)
    row_sum = keep(CHI, CUT, dtype=F32)
    phys_s = pltpu.SMEM((1, 1, 4), jnp.int32)
    virt_s = pltpu.SMEM((3, 1, 4), jnp.int32)
    env_v = keep(2, CHI, dtype=jnp.int32)
    arrivals = lambda n: pltpu.SemaphoreType.DMA((n,))
    own_left, own_top, sent_left, sent_top, corner_edge, corner_side, lay_a, lay_b = call(
        upper_kernel, "upper", [phys_charge, virt, site, env, ul, top, left, sketches],
        [tall_wide, tall_wide, tagged, tagged, broad, broad, lay, lay],
        [phys_s, virt_s, keep(27, 4, 3), env_v, keep(CHI, CHI), slabs, slabs, slabs, slabs, arrivals(9),
         slabs, slabs, slabs, wide, thin, row_sum, keep(LAY, LAY), keep(216, CHI, dtype=F32)],
        WORK[0], range(8),
    )
    before_range = from_behind(sent_top, "lx", 1)
    above_range = from_behind(sent_left, "ly", 1)
    others = [keep(CHI, CHI), slabs, slabs, slabs, arrivals(4), wide, thin]
    from_lower, sent_lower, lower_pair, rows_l = call(
        functools.partial(other_kernel, 1), "lower", [lay_b, ll, bottom, left, sketches],
        [tall_wide, tall, broad, tall], others, WORK[1], range(1, 5),
    )
    below = from_behind(sent_lower, "ly", -1)
    from_right, sent_right, right_pair, rows_t = call(
        functools.partial(other_kernel, 3), "right", [lay_a, ur, right, top, sketches],
        [tall_wide, tall, broad, tall], others, WORK[2], range(1, 5),
    )
    beside = from_behind(sent_right, "lx", -1)
    bond = [virt_s, env_v, arrivals(2), keep(2 * CUT, CHI, dtype=F32), slabs, slabs,
            keep(CHI, CUT), slabs, wide, thin, row_sum]
    lo, le, lu = call(
        functools.partial(bond_kernel, 0, 3), "left",
        [virt, env, own_left, from_lower, below, above_range, rows_l, lay_b, lower_pair, corner_edge],
        [corner, tall, corner], bond, WORK[3], range(2),
    )
    tr, te, tl = call(
        functools.partial(bond_kernel, 1, 2), "top",
        [virt, env, own_top, from_right, beside, before_range, rows_t, lay_a, right_pair, corner_side],
        [corner, tall, corner], bond, WORK[4], range(2),
    )
    lift = lambda a: a[None, None]
    edge = lambda a: a.reshape(D2, CHI, CHI).transpose(1, 0, 2)[None, None]
    return lift(lu), edge(le), lift(lo), lift(tl), edge(te), lift(tr)


def solution(mesh):
    split = lambda rest: P("lx", "ly", *([None] * rest))
    in_specs = tuple(split(rest) for rest in (5, 1, 2, 2, 2, 2, 2, 3, 3, 3, 3, 3))
    out_specs = tuple(split(rest) for rest in (2, 3, 2, 2, 3, 2))
    return jax.shard_map(shards, mesh=mesh, in_specs=in_specs, out_specs=out_specs, check_vma=False)
```

```python
import functools

import jax
import jax.numpy as jnp
from jax import lax
from jax.experimental import pallas as pl
from jax.experimental.pallas import tpu as pltpu
from jax.sharding import PartitionSpec as P

F32 = jnp.float32
BF16 = jnp.bfloat16
CHI = 128
D2 = 9
CUT = CHI * D2
TALL = CHI * 8
LAY = 96
GROUP = 32
CHUNKS = CHI // GROUP
ROWS = GROUP * 8
VMEM = 24 * 1024 * 1024
WORK = 10_000_000


def dot(a, b):
    return lax.dot_general(a, b, (((1,), (0,)), ((), ())), preferred_element_type=F32)


def dot_nt(a, b):
    return lax.dot_general(a, b, (((1,), (1,)), ((), ())), preferred_element_type=F32)


def dot_tn(a, b):
    return lax.dot_general(a, b, (((0,), (0,)), ((), ())), preferred_element_type=F32)


def exact_tn(a, b):
    return lax.dot_general(
        a, b, (((0,), (0,)), ((), ())), precision=lax.Precision.HIGHEST, preferred_element_type=F32
    )


def exact_nt(a, b):
    return lax.dot_general(
        a, b, (((1,), (1,)), ((), ())), precision=lax.Precision.HIGHEST, preferred_element_type=F32
    )


def slab(ref, p):
    return ref[p * CHI : (p + 1) * CHI, :]


def side_by_side(ref):
    return jnp.concatenate([slab(ref, p) for p in range(D2)], axis=1)


def pack_rows(slab_of, wide, out):
    for p in range(8):
        wide[pl.ds(p, CHI, stride=8), :] = slab_of(p).astype(F32)
    out[0:TALL, :] = wide[0:TALL, :].astype(BF16)
    out[TALL:CUT, :] = slab_of(8).astype(BF16)


def packed_slab(wide, p):
    return wide[pl.ds(p, CHI, stride=8), :] if p < 8 else wide[TALL:CUT, :]


def weave(one, steps_one, two, steps_two):
    done_one = done_two = 0
    live_one = live_two = True
    while live_one or live_two:
        if live_one and (not live_two or done_one * steps_two <= done_two * steps_one):
            live_one = next(one, "end") != "end"
            done_one += 1
        else:
            live_two = next(two, "end") != "end"
            done_two += 1


def run(steps):
    for _ in steps:
        pass


CHAIN_STEPS = 3 * CHUNKS + 2


def chain(left, right, layer, thin, consume):
    thin[...] = jnp.zeros_like(thin)
    last = dot(left[TALL:CUT, :], right[...])
    for q in range(D2):
        thin[pl.ds(q, CHI, stride=16), :] = last[:, q * CHI : (q + 1) * CHI]
    yield
    blank = jnp.zeros((8, CHI), F32)

    def product(chunk):
        return dot(left[chunk * ROWS : (chunk + 1) * ROWS, :], right[...])

    def mix(chunk, three):
        stacks = []
        for f in range(GROUP):
            here = (chunk * GROUP + f) * 16
            parts = [three[f * 8 : f * 8 + 8, q * CHI : (q + 1) * CHI] for q in range(D2)]
            stack = jnp.concatenate(parts + [thin[here : here + 16, :], blank], axis=0)
            stacks.append(stack.astype(BF16))
        return dot(layer[...], jnp.concatenate(stacks, axis=1))

    def hand_on(chunk, mixed):
        tall = []
        for f in range(GROUP):
            here = (chunk * GROUP + f) * 16
            lanes = slice(f * CHI, (f + 1) * CHI)
            thin[here : here + 16, :] = mixed[72:88, lanes]
            tall.append(
                jnp.concatenate([mixed[s * 8 : s * 8 + 8, lanes] for s in range(D2)], axis=1)
            )
        rows = slice(chunk * ROWS, (chunk + 1) * ROWS)
        consume(rows, jnp.concatenate(tall, axis=0).astype(BF16))

    three = product(0)
    before = None
    for chunk in range(CHUNKS):
        following = product(chunk + 1) if chunk + 1 < CHUNKS else None
        yield
        mixed = mix(chunk, three)
        yield
        if before is not None:
            hand_on(chunk - 1, before)
        yield
        before, three = mixed, following
    hand_on(CHUNKS - 1, before)
    rest = [thin[pl.ds(s, CHI, stride=16), :].astype(BF16) for s in range(D2)]
    consume(slice(TALL, CUT), jnp.concatenate(rest, axis=1))


def third(n):
    return (n * 11) >> 5


def layer_masks():
    row = lax.broadcasted_iota(jnp.int32, (LAY, 81), 0)
    lane = lax.broadcasted_iota(jnp.int32, (LAY, 81), 1)
    late = row >= 72
    slow = jnp.where(late, row - 72, row >> 3)
    fast = jnp.where(late, 8, row & 7)
    valid = row < 81
    pairs = ((third(slow), third(fast)), (slow - 3 * third(slow), fast - 3 * third(fast)))
    leg_l = (lane * 19) >> 9
    rest = lane - 27 * leg_l
    leg_u = (rest * 57) >> 9
    rest = rest - 9 * leg_u
    leg_r = (rest * 11) >> 5
    leg_d = rest - 3 * leg_r

    def mask(slow_leg, fast_leg):
        return [
            jnp.where(valid & (slow_leg == a) & (fast_leg == b), 1.0, 0.0).astype(F32)
            for a, b in pairs
        ]

    return mask(leg_r, leg_u), mask(leg_d, leg_l), mask(leg_r, leg_d), mask(leg_u, leg_l)


def kept_rows(site, phys, virt, corner):
    lane = lax.broadcasted_iota(jnp.int32, (8, 81), 1)
    state = lax.broadcasted_iota(jnp.int32, (8, 81), 0)
    leg_l = (lane * 19) >> 9
    rest = lane - 27 * leg_l
    leg_u = (rest * 57) >> 9
    rest = rest - 9 * leg_u
    leg_r = (rest * 11) >> 5
    leg_d = rest - 3 * leg_r
    total = jnp.zeros((8, 81), jnp.int32)
    for s in range(4):
        total = total + jnp.where(state == s, phys[0, 0, s], 0)
    for i in range(3):
        total = total + jnp.where(leg_l == i, virt[i, 0, 0], 0)
        total = total + jnp.where(leg_u == i, virt[i, 0, 1], 0)
        total = total - jnp.where(leg_r == i, virt[i, 0, 2], 0)
        total = total - jnp.where(leg_d == i, virt[i, 0, 3], 0)
    corner[...] = jnp.zeros_like(corner)
    for n in range(27):
        corner[8 * n : 8 * n + 4, 0:3] = site[n].astype(F32)
    lane = lax.broadcasted_iota(jnp.int32, (CHI, 81), 1)
    leg = lax.broadcasted_iota(jnp.int32, (CHI, 81), 0)
    place = jnp.where(lane - 3 * ((lane * 683) >> 11) == leg, 1.0, 0.0).astype(BF16)
    wide_site = dot(corner[...].astype(BF16), place)
    block = lax.broadcasted_iota(jnp.int32, (216, 81), 0) >> 3
    lane = lax.broadcasted_iota(jnp.int32, (216, 81), 1)
    wide_site = jnp.where((lane * 683) >> 11 == block, wide_site, 0.0)
    rows = wide_site[0:8]
    for n in range(1, 27):
        rows = rows + wide_site[8 * n : 8 * n + 8]
    return jnp.where(total == 0, rows, 0.0)


def build_layers(kept, out_a, out_b, out_c):
    m_ru, m_dl, m_rd, m_ul = layer_masks()

    def build(rows, cols):
        halves = []
        for half in range(2):
            tall = jnp.concatenate([rows[half] * kept[s : s + 1, :] for s in range(4)], axis=0)
            halves.append(dot_nt(tall.astype(BF16), cols[half].astype(BF16)))
        ket_bra = halves[0] * halves[1]
        total = ket_bra[:LAY]
        for s in range(1, 4):
            total = total + ket_bra[s * LAY : (s + 1) * LAY]
        return total.astype(BF16)

    out_a[...] = build(m_dl, m_ru)
    out_b[...] = build(m_ru, m_dl)
    out_c[...] = build(m_rd, m_ul)


def unpack_term(wide, term, sent):
    for p in range(D2):
        part = packed_slab(wide, p)
        term[p * CHI : (p + 1) * CHI, :] = part
        sent[p * CHI : (p + 1) * CHI, :] = part.astype(BF16)


def add_charges(sent, env, virt, leg):
    sent[CUT : CUT + 16, :] = jnp.concatenate(
        [env]
        + [
            jnp.full((1, CHI), (virt[p // 3, 0, leg] - virt[p % 3, 0, leg]).astype(F32))
            for p in range(D2)
        ]
        + [jnp.zeros((6, CHI), F32)],
        axis=0,
    ).astype(BF16)


def bring(sources, targets, arrived):
    copies = [
        pltpu.make_async_copy(source, target, arrived.at[i])
        for i, (source, target) in enumerate(zip(sources, targets))
    ]
    for copy in copies:
        copy.start()
    return copies


def right_kernel(
    phys_h, virt_h, site_h, corner_h, edge_h, edge_rows_h, sketches,
    term, sent, pair_out, rows_out, lay_a, lay_b, lay_c,
    phys, virt, site, corner, edge, edge_rows, sketch, arrived, wide, thin, small,
):
    copies = bring(
        (phys_h, virt_h, site_h, corner_h, edge_h, edge_rows_h, sketches.at[pl.ds(3 * CUT, CUT), :]),
        (phys, virt, site, corner, edge, edge_rows, sketch),
        arrived,
    )
    for copy in copies[:3]:
        copy.wait()
    build_layers(kept_rows(site, phys, virt, small), lay_a, lay_b, lay_c)
    sent[CUT : CUT + 32, :] = jnp.zeros((32, CHI), BF16)
    corner_product(copies[3:], corner, edge, edge_rows, sketch, lay_a, term, sent, pair_out, rows_out, wide, thin)


def lower_kernel(
    layer, corner_h, edge_h, edge_rows_h, sketches,
    term, sent, pair_out,
    corner, edge, edge_rows, sketch, arrived, wide, thin, rows_out,
):
    copies = bring(
        (corner_h, edge_h, edge_rows_h, sketches.at[pl.ds(CUT, CUT), :]),
        (corner, edge, edge_rows, sketch),
        arrived,
    )
    corner_product(copies, corner, edge, edge_rows, sketch, layer, term, sent, pair_out, rows_out, wide, thin)


def corner_product(
    copies, corner, edge, edge_rows, sketch, layer, term, sent, pair_out, rows_out, wide, thin
):
    for copy in copies[:3]:
        copy.wait()
    pair_out[...] = dot(corner[...], side_by_side(edge)).astype(BF16)
    pack_rows(lambda p: slab(edge_rows, p), wide, rows_out)
    copies[3].wait()

    def consume(rows, block):
        wide[rows, :] = dot(block, sketch[...])

    run(chain(rows_out, pair_out, layer, thin, consume))
    unpack_term(wide, term, sent)


def upper_kernel(
    lay_c, virt_h, env_h, corner_h, edge_t_h, edge_l_h, sketches,
    own_left, own_top, sent_left, sent_top, corner_edge, corner_side, left_rows,
    virt, env, corner, edge_t, edge_l, sketch_l, sketch_t, arrived,
    sketch_cols, sketch_rows, wide, thin, top_sum,
):
    first = sketches.at[pl.ds(0, CUT), :]
    third_one = sketches.at[pl.ds(2 * CUT, CUT), :]
    copies = bring(
        (virt_h, env_h, corner_h, edge_t_h, edge_l_h, first, third_one),
        (virt, env, corner, edge_t, edge_l, sketch_l, sketch_t),
        arrived,
    )
    for copy in copies[:5]:
        copy.wait()
    charges = env[...].astype(F32)
    add_charges(sent_left, charges[0:1], virt, 3)
    add_charges(sent_top, charges[1:2], virt, 2)
    corner_edge[...] = dot(corner[...], side_by_side(edge_t)).astype(BF16)
    corner_side[...] = dot_tn(corner[...], side_by_side(edge_l)).astype(BF16)
    pack_rows(lambda p: jnp.transpose(slab(edge_l, p).astype(F32)), wide, left_rows)
    copies[5].wait()
    wide[...] = sketch_l[...].astype(F32)
    for p in range(D2):
        sketch_cols[p * CHI : (p + 1) * CHI, :] = wide[pl.ds(p, CHI, stride=D2), :].astype(BF16)
    copies[6].wait()
    wide[...] = sketch_t[...].astype(F32)
    picked = [wide[pl.ds(p, CHI, stride=D2), :] for p in range(D2)]
    pack_rows(lambda p: picked[p], wide, sketch_rows)
    top_sum[...] = jnp.zeros_like(top_sum)

    def consume(rows, block):
        wide[rows, :] = dot(block, sketch_cols[...])
        top_sum[...] += dot_tn(sketch_rows[rows, :], block)

    run(chain(left_rows, corner_edge, lay_c, thin, consume))
    unpack_term(wide, own_left, sent_left)
    for p in range(D2):
        part = jnp.transpose(top_sum[:, p * CHI : (p + 1) * CHI])
        own_top[p * CHI : (p + 1) * CHI, :] = part
        sent_top[p * CHI : (p + 1) * CHI, :] = part.astype(BF16)


BLOCK = 32


def reciprocal(x):
    r = pl.reciprocal(x, approx=True)
    return r * (2.0 - x * r)


def spread(rows, p):
    return jnp.broadcast_to(rows[p : p + 1, :], (8, CHI))


STEPS = CHI // 2


def eliminate(grams, result):
    count = len(grams)
    sub = lax.broadcasted_iota(jnp.int32, (8, CHI), 0)
    lane = lax.broadcasted_iota(jnp.int32, (8, CHI), 1)
    groups = CHI // 8
    fact = [[g[8 * i : 8 * i + 8, :] for i in range(groups)] for g in grams]
    inv = [
        [jnp.where(lane == sub + 8 * i, 1.0, 0.0).astype(F32) for i in range(groups)] for _ in grams
    ]
    for start in range(0, groups, BLOCK // 8):
        end = start + BLOCK // 8
        for b in range(start, end):
            cols = [
                [
                    [
                        jnp.broadcast_to(fact[m][g][:, 8 * b + j : 8 * b + j + 1], (8, CHI))
                        for j in range(8)
                    ]
                    for g in range(b, end)
                ]
                for m in range(count)
            ]
            pivots = [jnp.zeros((8, CHI), F32) for _ in grams]
            for p in range(0, 8, 2):
                q = p + 1
                for m in range(count):
                    head = cols[m][0]
                    one, off, two = spread(head[p], p), spread(head[q], p), spread(head[q], q)
                    det = one * two - off * off
                    over_one, over_det = reciprocal(one), reciprocal(det)
                    lead = off * over_one
                    pivots[m] = jnp.where(
                        sub == p, one, jnp.where(sub == q, det * over_one, pivots[m])
                    )
                    later = range(q + 1, 8)
                    row_p = [spread(head[j], p) for j in later]
                    row_q = [spread(head[j], q) for j in later]
                    fact_p, fact_q = spread(fact[m][b], p), spread(fact[m][b], q)
                    inv_p, inv_q = spread(inv[m][b], p), spread(inv[m][b], q)
                    one_d, off_d, two_d = one * over_det, off * over_det, two * over_det
                    for g in range(b, end):
                        own = cols[m][g - b]
                        by_p = own[p] * two_d - own[q] * off_d
                        by_q = own[q] * one_d - own[p] * off_d
                        if g == b:
                            by_p = jnp.where(sub > q, by_p, jnp.where(sub == q, lead, 0.0))
                            by_q = jnp.where(sub > q, by_q, 0.0)
                        for n, j in enumerate(later):
                            own[j] = own[j] - by_p * row_p[n] - by_q * row_q[n]
                        fact[m][g] = fact[m][g] - by_p * fact_p - by_q * fact_q
                        inv[m][g] = inv[m][g] - by_p * inv_p - by_q * inv_q
                yield
            for m in range(count):
                root = lax.rsqrt(pivots[m])
                fact[m][b] = fact[m][b] * root
                inv[m][b] = inv[m][b] * root
        if end < groups:
            for m in range(count):
                upper = jnp.concatenate(fact[m][start:end], axis=0)
                both = jnp.concatenate([upper, jnp.concatenate(inv[m][start:end], axis=0)], axis=1)
                update = exact_tn(upper, both)
                for g in range(end, groups):
                    fact[m][g] = fact[m][g] - update[8 * g : 8 * g + 8, :CHI]
                    inv[m][g] = inv[m][g] - update[8 * g : 8 * g + 8, CHI:]
    result.extend(jnp.concatenate(i, axis=0) for i in inv)


def halves(values):
    high = values.astype(BF16)
    return high, (values - high.astype(F32)).astype(BF16)


def gram_of(ranged):
    high, low = halves(ranged)
    cross = dot_tn(high, low)
    return dot_tn(high, high) + (cross + jnp.transpose(cross))


def times_inverse(ranged, inverse):
    high, low = halves(ranged)
    inv_high, inv_low = halves(inverse)
    return dot_nt(high, inv_high) + (dot_nt(high, inv_low) + dot_nt(low, inv_high))


def unit(values):
    square = jnp.sum(jnp.sum(values * values, axis=1, keepdims=True), axis=0, keepdims=True)
    return (values / jnp.sqrt(square / values.size + 1e-06)).astype(BF16)


def slab_rows(wide_ref, p):
    return wide_ref[:, p * CHI : (p + 1) * CHI]


def corner_from(projector, pair):
    tall = jnp.concatenate([slab_rows(pair, p) for p in range(D2)], axis=0)
    return dot_tn(projector[...], tall)


def range_and_gram(own, other, tagged, ranged):
    row = lax.broadcasted_iota(jnp.int32, (CHI, CHI), 0)
    col = lax.broadcasted_iota(jnp.int32, (CHI, CHI), 1)
    tags = tagged[CUT : CUT + 16, :].astype(F32)
    across = jnp.broadcast_to(tags[0:1], (CHI, CHI))
    gap = across - jnp.transpose(across)
    for p in range(D2):
        sums = slab(own, p) + slab(other, p).astype(F32)
        ranged[p * CHI : (p + 1) * CHI, :] = jnp.where(gap == tags[1 + p : 2 + p], sums, 0.0)
    gram = gram_of(ranged[...])
    diagonal = jnp.where(row == col, gram, 0.0)
    mean = jnp.sum(jnp.sum(diagonal, axis=1, keepdims=True), axis=0, keepdims=True) / CHI
    return gram + jnp.where(row == col, 0.01 * mean + 1e-06, 0.0)


def early_kernel(
    from_lower, above_range, own_top, sent_top, beside,
    above, top,
    range_a, range_t,
):
    grams = [
        range_and_gram(from_lower, above_range, above_range, range_a),
        range_and_gram(own_top, beside, sent_top, range_t),
    ]
    inverses = []
    run(eliminate(grams, inverses))
    above[...] = times_inverse(range_a[...], inverses[0]).astype(BF16)
    top[...] = times_inverse(range_t[...], inverses[1]).astype(BF16)


def late_kernel(
    own_left, sent_left, below, from_right, before_range, above, top,
    left_rows, rows_t, lay_c, lay_a, corner_edge, corner_side, lower_pair, right_pair,
    out_lu, out_le, out_ll, out_tl, out_te, out_tr,
    range_l, range_b, left, before, beside_a, beside_t, mixed_l, mixed_t, packed, wide, thin_l, thin_t,
):
    grams = [
        range_and_gram(own_left, below, sent_left, range_l),
        range_and_gram(from_right, before_range, before_range, range_b),
    ]

    def keep_l(rows, block):
        mixed_l[rows, :] = block

    def keep_t(rows, block):
        mixed_t[rows, :] = block

    def products():
        beside_t[...] = side_by_side(top)
        yield from chain(rows_t, beside_t, lay_a, thin_t, keep_t)
        beside_a[...] = side_by_side(above)
        yield from chain(left_rows, beside_a, lay_c, thin_l, keep_l)
        out_lu[...] = unit(corner_from(above, corner_edge))
        out_tr[...] = unit(corner_from(top, right_pair))

    inverses = []
    weave(eliminate(grams, inverses), STEPS, products(), 2 * CHAIN_STEPS)
    left[...] = times_inverse(range_l[...], inverses[0]).astype(BF16)
    before[...] = times_inverse(range_b[...], inverses[1]).astype(BF16)
    out_ll[...] = unit(corner_from(left, lower_pair))
    out_tl[...] = unit(jnp.transpose(corner_from(before, corner_side)))
    pack_rows(lambda p: slab(left, p), wide, packed)
    result = unit(dot_tn(packed[...], mixed_l[...]))
    for p in range(D2):
        part = result[:, p * CHI : (p + 1) * CHI]
        out_le[p * CHI : (p + 1) * CHI, :] = jnp.transpose(part)
    pack_rows(lambda p: slab(before, p), wide, packed)
    result = unit(dot_tn(packed[...], mixed_t[...]))
    for p in range(D2):
        out_te[p * CHI : (p + 1) * CHI, :] = result[:, p * CHI : (p + 1) * CHI]


def shape(*dims, dtype=BF16):
    return jax.ShapeDtypeStruct(dims, dtype)


def call(body, name, ins, outs, scratch, far=()):
    moved = sum(a.size * a.dtype.itemsize for a in ins) + sum(
        o.size * jnp.dtype(o.dtype).itemsize for o in outs
    )
    whole = pl.BlockSpec(memory_space=pltpu.VMEM)
    return pl.pallas_call(
        body,
        name=name,
        out_shape=tuple(outs),
        in_specs=[
            pl.BlockSpec(memory_space=pltpu.HBM) if i in far else whole for i in range(len(ins))
        ],
        out_specs=(whole,) * len(outs),
        scratch_shapes=scratch,
        compiler_params=pltpu.CompilerParams(vmem_limit_bytes=VMEM if name != "right" else 60 * 1024 * 1024),
        cost_estimate=pl.CostEstimate(flops=1, bytes_accessed=1, transcendentals=0),
    )(*ins)


def from_behind(block, axis, distance):
    size = lax.axis_size(axis)
    route = [((i - distance) % size, i) for i in range(size)]
    return lax.ppermute(block, axis, route)


def flat(edge):
    return edge.transpose(1, 0, 2).reshape(CUT, CHI)


def shards(
    site_tensor, phys_charge, virt_charge, env_charge, corner_ul, corner_ur, corner_ll,
    edge_top, edge_right, edge_bottom, edge_left, sketch,
):
    site = site_tensor.transpose(0, 1, 3, 4, 5, 2, 6).reshape(27, 4, 3)
    virt = virt_charge.transpose(0, 3, 1, 2).reshape(3, 1, 4)
    env = env_charge[0, 0]
    ul, ur, ll = corner_ul[0, 0], corner_ur[0, 0], corner_ll[0, 0]
    top, right, bottom, left = (
        flat(e[0, 0]) for e in (edge_top, edge_right, edge_bottom, edge_left)
    )
    sketches = sketch[0, 0].reshape(4 * CUT, CHI)
    tall = shape(CUT, CHI)
    tall_wide = shape(CUT, CHI, dtype=F32)
    tagged = shape(CUT + 16, CHI)
    broad = shape(CHI, CUT)
    lay = shape(LAY, LAY)
    corner = shape(CHI, CHI)
    keep = lambda *dims, dtype=BF16: pltpu.VMEM(dims, dtype)
    slabs = keep(CUT, CHI)
    wide = keep(CUT, CHI, dtype=F32)
    thin = keep(CHI * 16, CHI, dtype=F32)
    row_sum = keep(CHI, CUT, dtype=F32)
    phys_s = pltpu.SMEM((1, 1, 4), jnp.int32)
    virt_s = pltpu.SMEM((3, 1, 4), jnp.int32)
    env_v = keep(2, CHI, dtype=jnp.int32)
    arrivals = lambda n: pltpu.SemaphoreType.DMA((n,))
    from_right, sent_right, right_pair, rows_t, lay_a, lay_b, lay_c = call(
        right_kernel, "right", [phys_charge, virt, site, ur, right, top, sketches],
        [tall_wide, shape(CUT + 32, CHI), broad, tall, lay, lay, lay],
        [phys_s, virt_s, keep(27, 4, 3), keep(CHI, CHI), slabs, slabs, slabs, arrivals(7), wide, thin,
         keep(216, CHI, dtype=F32)],
        range(7),
    )
    beside = from_behind(sent_right, "lx", -1)
    own_left, own_top, sent_left, sent_top, corner_edge, corner_side, left_rows = call(
        upper_kernel, "upper", [lay_c, virt, env, ul, top, left, sketches],
        [tall_wide, tall_wide, tagged, tagged, broad, broad, tall],
        [virt_s, env_v, keep(CHI, CHI), slabs, slabs, slabs, slabs, arrivals(7),
         slabs, slabs, wide, thin, row_sum],
        range(1, 7),
    )
    above_range = from_behind(sent_left, "ly", 1)
    before_range = from_behind(sent_top, "lx", 1)
    from_lower, sent_lower, lower_pair = call(
        lower_kernel, "lower", [lay_b, ll, bottom, left, sketches],
        [tall_wide, tall, broad], [keep(CHI, CHI), slabs, slabs, slabs, arrivals(4), wide, thin, slabs],
        range(1, 5),
    )
    below = from_behind(sent_lower, "ly", -1)
    above, top_basis = call(
        early_kernel, "early", [from_lower, above_range, own_top, sent_top, beside],
        [tall, tall], [wide, wide],
    )
    square = keep(CUT, CUT)
    lu, le, lo, tl, te, tr = call(
        late_kernel, "late",
        [own_left, sent_left, below, from_right, before_range, above, top_basis, left_rows, rows_t,
         lay_c, lay_a, corner_edge, corner_side, lower_pair, right_pair],
        [corner, tall, corner, corner, tall, corner],
        [wide, wide, slabs, slabs, keep(CHI, CUT), keep(CHI, CUT), square, square, slabs, wide, thin, thin],
    )
    lift = lambda a: a[None, None]
    edge = lambda a: a.reshape(D2, CHI, CHI).transpose(1, 0, 2)[None, None]
    return lift(lu), edge(le), lift(lo), lift(tl), edge(te), lift(tr)


def solution(mesh):
    split = lambda rest: P("lx", "ly", *([None] * rest))
    in_specs = tuple(split(rest) for rest in (5, 1, 2, 2, 2, 2, 2, 3, 3, 3, 3, 3))
    out_specs = tuple(split(rest) for rest in (2, 3, 2, 2, 3, 2))
    return jax.shard_map(shards, mesh=mesh, in_specs=in_specs, out_specs=out_specs, check_vma=False)
```

```python
import functools

import jax
import jax.numpy as jnp
from jax import lax
from jax.experimental import pallas as pl
from jax.experimental.pallas import tpu as pltpu
from jax.sharding import PartitionSpec as P

F32 = jnp.float32
BF16 = jnp.bfloat16
CHI = 128
D2 = 9
CUT = CHI * D2
TALL = CHI * 8
LAY = 96
GROUP = 32
CHUNKS = CHI // GROUP
ROWS = GROUP * 8
VMEM = 24 * 1024 * 1024
WORK = 10_000_000


def dot(a, b):
    return lax.dot_general(a, b, (((1,), (0,)), ((), ())), preferred_element_type=F32)


def dot_nt(a, b):
    return lax.dot_general(a, b, (((1,), (1,)), ((), ())), preferred_element_type=F32)


def dot_tn(a, b):
    return lax.dot_general(a, b, (((0,), (0,)), ((), ())), preferred_element_type=F32)


def exact_tn(a, b):
    return lax.dot_general(
        a, b, (((0,), (0,)), ((), ())), precision=lax.Precision.HIGHEST, preferred_element_type=F32
    )


def exact_nt(a, b):
    return lax.dot_general(
        a, b, (((1,), (1,)), ((), ())), precision=lax.Precision.HIGHEST, preferred_element_type=F32
    )


def slab(ref, p):
    return ref[p * CHI : (p + 1) * CHI, :]


def side_by_side(ref):
    return jnp.concatenate([slab(ref, p) for p in range(D2)], axis=1)


def pack_rows(slab_of, wide, out):
    for p in range(8):
        wide[pl.ds(p, CHI, stride=8), :] = slab_of(p).astype(F32)
    out[0:TALL, :] = wide[0:TALL, :].astype(BF16)
    out[TALL:CUT, :] = slab_of(8).astype(BF16)


def packed_slab(wide, p):
    return wide[pl.ds(p, CHI, stride=8), :] if p < 8 else wide[TALL:CUT, :]


def weave(one, steps_one, two, steps_two):
    done_one = done_two = 0
    live_one = live_two = True
    while live_one or live_two:
        if live_one and (not live_two or done_one * steps_two <= done_two * steps_one):
            live_one = next(one, "end") != "end"
            done_one += 1
        else:
            live_two = next(two, "end") != "end"
            done_two += 1


def run(steps):
    for _ in steps:
        pass


CHAIN_STEPS = 3 * CHUNKS + 2


def chain(left, right, layer, thin, consume):
    thin[...] = jnp.zeros_like(thin)
    last = dot(left[TALL:CUT, :], right[...])
    for q in range(D2):
        thin[pl.ds(q, CHI, stride=16), :] = last[:, q * CHI : (q + 1) * CHI]
    yield
    blank = jnp.zeros((8, CHI), F32)

    def product(chunk):
        return dot(left[chunk * ROWS : (chunk + 1) * ROWS, :], right[...])

    def mix(chunk, three):
        stacks = []
        for f in range(GROUP):
            here = (chunk * GROUP + f) * 16
            parts = [three[f * 8 : f * 8 + 8, q * CHI : (q + 1) * CHI] for q in range(D2)]
            stack = jnp.concatenate(parts + [thin[here : here + 16, :], blank], axis=0)
            stacks.append(stack.astype(BF16))
        return dot(layer[...], jnp.concatenate(stacks, axis=1))

    def hand_on(chunk, mixed):
        tall = []
        for f in range(GROUP):
            here = (chunk * GROUP + f) * 16
            lanes = slice(f * CHI, (f + 1) * CHI)
            thin[here : here + 16, :] = mixed[72:88, lanes]
            tall.append(
                jnp.concatenate([mixed[s * 8 : s * 8 + 8, lanes] for s in range(D2)], axis=1)
            )
        rows = slice(chunk * ROWS, (chunk + 1) * ROWS)
        consume(rows, jnp.concatenate(tall, axis=0).astype(BF16))

    three = product(0)
    before = None
    for chunk in range(CHUNKS):
        following = product(chunk + 1) if chunk + 1 < CHUNKS else None
        yield
        mixed = mix(chunk, three)
        yield
        if before is not None:
            hand_on(chunk - 1, before)
        yield
        before, three = mixed, following
    hand_on(CHUNKS - 1, before)
    rest = [thin[pl.ds(s, CHI, stride=16), :].astype(BF16) for s in range(D2)]
    consume(slice(TALL, CUT), jnp.concatenate(rest, axis=1))


def third(n):
    return (n * 11) >> 5


def layer_masks():
    row = lax.broadcasted_iota(jnp.int32, (LAY, 81), 0)
    lane = lax.broadcasted_iota(jnp.int32, (LAY, 81), 1)
    late = row >= 72
    slow = jnp.where(late, row - 72, row >> 3)
    fast = jnp.where(late, 8, row & 7)
    valid = row < 81
    pairs = ((third(slow), third(fast)), (slow - 3 * third(slow), fast - 3 * third(fast)))
    leg_l = (lane * 19) >> 9
    rest = lane - 27 * leg_l
    leg_u = (rest * 57) >> 9
    rest = rest - 9 * leg_u
    leg_r = (rest * 11) >> 5
    leg_d = rest - 3 * leg_r

    def mask(slow_leg, fast_leg):
        return [
            jnp.where(valid & (slow_leg == a) & (fast_leg == b), 1.0, 0.0).astype(F32)
            for a, b in pairs
        ]

    return mask(leg_r, leg_u), mask(leg_d, leg_l), mask(leg_r, leg_d), mask(leg_u, leg_l)


def kept_rows(site, phys, virt, corner):
    lane = lax.broadcasted_iota(jnp.int32, (8, 81), 1)
    state = lax.broadcasted_iota(jnp.int32, (8, 81), 0)
    leg_l = (lane * 19) >> 9
    rest = lane - 27 * leg_l
    leg_u = (rest * 57) >> 9
    rest = rest - 9 * leg_u
    leg_r = (rest * 11) >> 5
    leg_d = rest - 3 * leg_r
    total = jnp.zeros((8, 81), jnp.int32)
    for s in range(4):
        total = total + jnp.where(state == s, phys[0, 0, s], 0)
    for i in range(3):
        total = total + jnp.where(leg_l == i, virt[i, 0, 0], 0)
        total = total + jnp.where(leg_u == i, virt[i, 0, 1], 0)
        total = total - jnp.where(leg_r == i, virt[i, 0, 2], 0)
        total = total - jnp.where(leg_d == i, virt[i, 0, 3], 0)
    corner[...] = jnp.zeros_like(corner)
    for n in range(27):
        corner[8 * n : 8 * n + 4, 0:3] = site[n].astype(F32)
    lane = lax.broadcasted_iota(jnp.int32, (CHI, 81), 1)
    leg = lax.broadcasted_iota(jnp.int32, (CHI, 81), 0)
    place = jnp.where(lane - 3 * ((lane * 683) >> 11) == leg, 1.0, 0.0).astype(BF16)
    wide_site = dot(corner[...].astype(BF16), place)
    block = lax.broadcasted_iota(jnp.int32, (216, 81), 0) >> 3
    lane = lax.broadcasted_iota(jnp.int32, (216, 81), 1)
    wide_site = jnp.where((lane * 683) >> 11 == block, wide_site, 0.0)
    rows = wide_site[0:8]
    for n in range(1, 27):
        rows = rows + wide_site[8 * n : 8 * n + 8]
    return jnp.where(total == 0, rows, 0.0)


def build_layers(kept, *wanted):
    masks = dict(zip(("ru", "dl", "rd", "ul"), layer_masks()))

    for out, rows, cols in wanted:
        halves_of = []
        for half in range(2):
            tall = jnp.concatenate(
                [masks[rows][half] * kept[s : s + 1, :] for s in range(4)], axis=0
            )
            halves_of.append(dot_nt(tall.astype(BF16), masks[cols][half].astype(BF16)))
        ket_bra = halves_of[0] * halves_of[1]
        total = ket_bra[:LAY]
        for s in range(1, 4):
            total = total + ket_bra[s * LAY : (s + 1) * LAY]
        out[...] = total.astype(BF16)


def unpack_term(wide, term, sent):
    for p in range(D2):
        part = packed_slab(wide, p)
        term[p * CHI : (p + 1) * CHI, :] = part
        sent[p * CHI : (p + 1) * CHI, :] = part.astype(BF16)


def add_charges(sent, env, virt, leg):
    sent[CUT : CUT + 16, :] = jnp.concatenate(
        [env]
        + [
            jnp.full((1, CHI), (virt[p // 3, 0, leg] - virt[p % 3, 0, leg]).astype(F32))
            for p in range(D2)
        ]
        + [jnp.zeros((6, CHI), F32)],
        axis=0,
    ).astype(BF16)


def bring(sources, targets, arrived):
    copies = [
        pltpu.make_async_copy(source, target, arrived.at[i])
        for i, (source, target) in enumerate(zip(sources, targets))
    ]
    for copy in copies:
        copy.start()
    return copies


def right_kernel(
    phys_h, virt_h, site_h, corner_h, edge_h, edge_rows_h, sketches,
    term, sent, pair_out, rows_out, lay_a, lay_b,
    phys, virt, site, corner, edge, edge_rows, sketch, arrived, wide, thin, small,
):
    copies = bring(
        (phys_h, virt_h, site_h, corner_h, edge_h, edge_rows_h, sketches.at[pl.ds(3 * CUT, CUT), :]),
        (phys, virt, site, corner, edge, edge_rows, sketch),
        arrived,
    )
    for copy in copies[:3]:
        copy.wait()
    kept = kept_rows(site, phys, virt, small)
    for copy in copies[3:]:
        copy.wait()
    build_layers(kept, (lay_a, "dl", "ru"), (lay_b, "ru", "dl"))
    sent[CUT : CUT + 32, :] = jnp.zeros((32, CHI), BF16)
    corner_product((), corner, edge, edge_rows, sketch, lay_a, term, sent, pair_out, rows_out, wide, thin)


def lower_kernel(
    layer, corner_h, edge_h, edge_rows_h, sketches,
    term, sent, pair_out,
    corner, edge, edge_rows, sketch, arrived, wide, thin, rows_out,
):
    copies = bring(
        (corner_h, edge_h, edge_rows_h, sketches.at[pl.ds(CUT, CUT), :]),
        (corner, edge, edge_rows, sketch),
        arrived,
    )
    corner_product(copies, corner, edge, edge_rows, sketch, layer, term, sent, pair_out, rows_out, wide, thin)


def corner_product(
    copies, corner, edge, edge_rows, sketch, layer, term, sent, pair_out, rows_out, wide, thin
):
    for copy in copies[:2]:
        copy.wait()
    pair_out[...] = dot(corner[...], side_by_side(edge)).astype(BF16)
    for copy in copies[2:]:
        copy.wait()
    pack_rows(lambda p: slab(edge_rows, p), wide, rows_out)

    def consume(rows, block):
        wide[rows, :] = dot(block, sketch[...])

    run(chain(rows_out, pair_out, layer, thin, consume))
    unpack_term(wide, term, sent)


def upper_kernel(
    phys_h, virt_h, site_h, env_h, corner_h, edge_t_h, edge_l_h, sketches,
    own_left, own_top, sent_left, sent_top, corner_edge, corner_side, left_rows, lay_c,
    phys, virt, site, env, corner, edge_t, edge_l, sketch_l, sketch_t, arrived,
    sketch_cols, sketch_rows, wide, thin, top_sum, small,
):
    first = sketches.at[pl.ds(0, CUT), :]
    third_one = sketches.at[pl.ds(2 * CUT, CUT), :]
    copies = bring(
        (corner_h, edge_t_h, edge_l_h, phys_h, virt_h, site_h, env_h, first, third_one),
        (corner, edge_t, edge_l, phys, virt, site, env, sketch_l, sketch_t),
        arrived,
    )
    top_sum[...] = jnp.zeros_like(top_sum)
    for copy in copies:
        copy.wait()
    kept = kept_rows(site, phys, virt, small)
    charges = env[...].astype(F32)
    add_charges(sent_left, charges[0:1], virt, 3)
    add_charges(sent_top, charges[1:2], virt, 2)
    corner_edge[...] = dot(corner[...], side_by_side(edge_t)).astype(BF16)
    corner_side[...] = dot_tn(corner[...], side_by_side(edge_l)).astype(BF16)
    build_layers(kept, (lay_c, "rd", "ul"))
    pack_rows(lambda p: jnp.transpose(slab(edge_l, p).astype(F32)), wide, left_rows)
    wide[...] = sketch_l[...].astype(F32)
    for p in range(D2):
        sketch_cols[p * CHI : (p + 1) * CHI, :] = wide[pl.ds(p, CHI, stride=D2), :].astype(BF16)
    wide[...] = sketch_t[...].astype(F32)
    picked = [wide[pl.ds(p, CHI, stride=D2), :] for p in range(D2)]
    pack_rows(lambda p: picked[p], wide, sketch_rows)

    def consume(rows, block):
        wide[rows, :] = dot(block, sketch_cols[...])
        top_sum[...] += dot_tn(sketch_rows[rows, :], block)

    run(chain(left_rows, corner_edge, lay_c, thin, consume))
    unpack_term(wide, own_left, sent_left)
    for p in range(D2):
        part = jnp.transpose(top_sum[:, p * CHI : (p + 1) * CHI])
        own_top[p * CHI : (p + 1) * CHI, :] = part
        sent_top[p * CHI : (p + 1) * CHI, :] = part.astype(BF16)


BLOCK = 32


def reciprocal(x):
    r = pl.reciprocal(x, approx=True)
    return r * (2.0 - x * r)


def spread(rows, p):
    return jnp.broadcast_to(rows[p : p + 1, :], (8, CHI))


STEPS = CHI // 2


def eliminate(grams, result):
    count = len(grams)
    sub = lax.broadcasted_iota(jnp.int32, (8, CHI), 0)
    lane = lax.broadcasted_iota(jnp.int32, (8, CHI), 1)
    groups = CHI // 8
    fact = [[g[8 * i : 8 * i + 8, :] for i in range(groups)] for g in grams]
    inv = [
        [jnp.where(lane == sub + 8 * i, 1.0, 0.0).astype(F32) for i in range(groups)] for _ in grams
    ]
    for start in range(0, groups, BLOCK // 8):
        end = start + BLOCK // 8
        for b in range(start, end):
            cols = [
                [
                    [
                        jnp.broadcast_to(fact[m][g][:, 8 * b + j : 8 * b + j + 1], (8, CHI))
                        for j in range(8)
                    ]
                    for g in range(b, end)
                ]
                for m in range(count)
            ]
            pivots = [jnp.zeros((8, CHI), F32) for _ in grams]
            for p in range(0, 8, 2):
                q = p + 1
                for m in range(count):
                    head = cols[m][0]
                    one, off, two = spread(head[p], p), spread(head[q], p), spread(head[q], q)
                    det = one * two - off * off
                    over_one, over_det = reciprocal(one), reciprocal(det)
                    lead = off * over_one
                    pivots[m] = jnp.where(
                        sub == p, one, jnp.where(sub == q, det * over_one, pivots[m])
                    )
                    later = range(q + 1, 8)
                    row_p = [spread(head[j], p) for j in later]
                    row_q = [spread(head[j], q) for j in later]
                    fact_p, fact_q = spread(fact[m][b], p), spread(fact[m][b], q)
                    inv_p, inv_q = spread(inv[m][b], p), spread(inv[m][b], q)
                    one_d, off_d, two_d = one * over_det, off * over_det, two * over_det
                    for g in range(b, end):
                        own = cols[m][g - b]
                        by_p = own[p] * two_d - own[q] * off_d
                        by_q = own[q] * one_d - own[p] * off_d
                        if g == b:
                            by_p = jnp.where(sub > q, by_p, jnp.where(sub == q, lead, 0.0))
                            by_q = jnp.where(sub > q, by_q, 0.0)
                        for n, j in enumerate(later):
                            own[j] = own[j] - by_p * row_p[n] - by_q * row_q[n]
                        fact[m][g] = fact[m][g] - by_p * fact_p - by_q * fact_q
                        inv[m][g] = inv[m][g] - by_p * inv_p - by_q * inv_q
                yield
            for m in range(count):
                root = lax.rsqrt(pivots[m])
                fact[m][b] = fact[m][b] * root
                inv[m][b] = inv[m][b] * root
        if end < groups:
            for m in range(count):
                upper = jnp.concatenate(fact[m][start:end], axis=0)
                both = jnp.concatenate([upper, jnp.concatenate(inv[m][start:end], axis=0)], axis=1)
                update = exact_tn(upper, both)
                for g in range(end, groups):
                    fact[m][g] = fact[m][g] - update[8 * g : 8 * g + 8, :CHI]
                    inv[m][g] = inv[m][g] - update[8 * g : 8 * g + 8, CHI:]
    result.extend(jnp.concatenate(i, axis=0) for i in inv)


def halves(values):
    high = values.astype(BF16)
    return high, (values - high.astype(F32)).astype(BF16)


def gram_of(ranged):
    high, low = halves(ranged)
    both = dot_tn(high, jnp.concatenate([high, low], axis=1))
    cross = both[:, CHI:]
    return both[:, :CHI] + (cross + jnp.transpose(cross))


def times_inverse(ranged, inverse):
    high, low = halves(ranged)
    inv_high, inv_low = halves(inverse)
    factors = jnp.concatenate(
        [
            jnp.concatenate([inv_high, inv_high], axis=1),
            jnp.concatenate([inv_low, jnp.zeros_like(inv_low)], axis=1),
        ],
        axis=0,
    )
    both = dot_nt(jnp.concatenate([high, low], axis=1), factors)
    return both[:, :CHI] + both[:, CHI:]


def unit(values):
    square = jnp.sum(jnp.sum(values * values, axis=1, keepdims=True), axis=0, keepdims=True)
    return (values / jnp.sqrt(square / values.size + 1e-06)).astype(BF16)


def slab_rows(wide_ref, p):
    return wide_ref[:, p * CHI : (p + 1) * CHI]


def corner_from(projector, pair):
    tall = jnp.concatenate([slab_rows(pair, p) for p in range(D2)], axis=0)
    return dot_tn(projector[...], tall)


def range_and_gram(own, other, tagged, ranged):
    row = lax.broadcasted_iota(jnp.int32, (CHI, CHI), 0)
    col = lax.broadcasted_iota(jnp.int32, (CHI, CHI), 1)
    tags = tagged[CUT : CUT + 16, :].astype(F32)
    across = jnp.broadcast_to(tags[0:1], (CHI, CHI))
    gap = across - jnp.transpose(across)
    for p in range(D2):
        sums = slab(own, p) + slab(other, p).astype(F32)
        ranged[p * CHI : (p + 1) * CHI, :] = jnp.where(gap == tags[1 + p : 2 + p], sums, 0.0)
    gram = gram_of(ranged[...])
    diagonal = jnp.where(row == col, gram, 0.0)
    mean = jnp.sum(jnp.sum(diagonal, axis=1, keepdims=True), axis=0, keepdims=True) / CHI
    return gram + jnp.where(row == col, 0.01 * mean + 1e-06, 0.0)


def early_kernel(
    from_lower, above_range, own_top, sent_top, beside,
    above, top,
    range_a, range_t,
):
    grams = [
        range_and_gram(from_lower, above_range, above_range, range_a),
        range_and_gram(own_top, beside, sent_top, range_t),
    ]
    inverses = []
    run(eliminate(grams, inverses))
    above[...] = times_inverse(range_a[...], inverses[0]).astype(BF16)
    top[...] = times_inverse(range_t[...], inverses[1]).astype(BF16)


def late_kernel(
    own_left, sent_left, below, from_right, before_range, above, top,
    left_rows, rows_t, lay_c, lay_a, corner_edge, corner_side, lower_pair, right_pair,
    out_lu, out_le, out_ll, out_tl, out_te, out_tr,
    range_l, range_b, left, before, beside_a, beside_t, mixed_l, mixed_t, packed, wide, thin_l, thin_t,
):
    grams = [
        range_and_gram(own_left, below, sent_left, range_l),
        range_and_gram(from_right, before_range, before_range, range_b),
    ]

    def keep_l(rows, block):
        mixed_l[rows, :] = block

    def keep_t(rows, block):
        mixed_t[rows, :] = block

    def products():
        beside_t[...] = side_by_side(top)
        yield from chain(rows_t, beside_t, lay_a, thin_t, keep_t)
        beside_a[...] = side_by_side(above)
        yield from chain(left_rows, beside_a, lay_c, thin_l, keep_l)
        out_lu[...] = unit(corner_from(above, corner_edge))
        out_tr[...] = unit(corner_from(top, right_pair))

    inverses = []
    weave(eliminate(grams, inverses), STEPS, products(), 2 * CHAIN_STEPS)
    left[...] = times_inverse(range_l[...], inverses[0]).astype(BF16)
    before[...] = times_inverse(range_b[...], inverses[1]).astype(BF16)
    out_ll[...] = unit(corner_from(left, lower_pair))
    out_tl[...] = unit(jnp.transpose(corner_from(before, corner_side)))
    pack_rows(lambda p: slab(left, p), wide, packed)
    result = unit(dot_tn(packed[...], mixed_l[...]))
    for p in range(D2):
        part = result[:, p * CHI : (p + 1) * CHI]
        out_le[p * CHI : (p + 1) * CHI, :] = jnp.transpose(part)
    pack_rows(lambda p: slab(before, p), wide, packed)
    result = unit(dot_tn(packed[...], mixed_t[...]))
    for p in range(D2):
        out_te[p * CHI : (p + 1) * CHI, :] = result[:, p * CHI : (p + 1) * CHI]


def shape(*dims, dtype=BF16):
    return jax.ShapeDtypeStruct(dims, dtype)


def call(body, name, ins, outs, scratch, far=()):
    moved = sum(a.size * a.dtype.itemsize for a in ins) + sum(
        o.size * jnp.dtype(o.dtype).itemsize for o in outs
    )
    whole = pl.BlockSpec(memory_space=pltpu.VMEM)
    return pl.pallas_call(
        body,
        name=name,
        out_shape=tuple(outs),
        in_specs=[
            pl.BlockSpec(memory_space=pltpu.HBM) if i in far else whole for i in range(len(ins))
        ],
        out_specs=(whole,) * len(outs),
        scratch_shapes=scratch,
        compiler_params=pltpu.CompilerParams(vmem_limit_bytes=VMEM if name != "right" else 60 * 1024 * 1024),
        cost_estimate=pl.CostEstimate(flops=1, bytes_accessed=1, transcendentals=0),
    )(*ins)


def from_behind(block, axis, distance):
    size = lax.axis_size(axis)
    route = [((i - distance) % size, i) for i in range(size)]
    return lax.ppermute(block, axis, route)


def flat(edge):
    return edge.transpose(1, 0, 2).reshape(CUT, CHI)


def shards(
    site_tensor, phys_charge, virt_charge, env_charge, corner_ul, corner_ur, corner_ll,
    edge_top, edge_right, edge_bottom, edge_left, sketch,
):
    site = site_tensor.transpose(0, 1, 3, 4, 5, 2, 6).reshape(27, 4, 3)
    virt = virt_charge.transpose(0, 3, 1, 2).reshape(3, 1, 4)
    env = env_charge[0, 0]
    ul, ur, ll = corner_ul[0, 0], corner_ur[0, 0], corner_ll[0, 0]
    top, right, bottom, left = (
        flat(e[0, 0]) for e in (edge_top, edge_right, edge_bottom, edge_left)
    )
    sketches = sketch[0, 0].reshape(4 * CUT, CHI)
    tall = shape(CUT, CHI)
    tall_wide = shape(CUT, CHI, dtype=F32)
    tagged = shape(CUT + 16, CHI)
    broad = shape(CHI, CUT)
    lay = shape(LAY, LAY)
    corner = shape(CHI, CHI)
    keep = lambda *dims, dtype=BF16: pltpu.VMEM(dims, dtype)
    slabs = keep(CUT, CHI)
    wide = keep(CUT, CHI, dtype=F32)
    thin = keep(CHI * 16, CHI, dtype=F32)
    row_sum = keep(CHI, CUT, dtype=F32)
    phys_s = pltpu.SMEM((1, 1, 4), jnp.int32)
    virt_s = pltpu.SMEM((3, 1, 4), jnp.int32)
    env_v = keep(2, CHI, dtype=jnp.int32)
    arrivals = lambda n: pltpu.SemaphoreType.DMA((n,))
    from_right, sent_right, right_pair, rows_t, lay_a, lay_b = call(
        right_kernel, "right", [phys_charge, virt, site, ur, right, top, sketches],
        [tall_wide, shape(CUT + 32, CHI), broad, tall, lay, lay],
        [phys_s, virt_s, keep(27, 4, 3), keep(CHI, CHI), slabs, slabs, slabs, arrivals(7), wide, thin,
         keep(216, CHI, dtype=F32)],
        range(7),
    )
    beside = from_behind(sent_right, "lx", -1)
    own_left, own_top, sent_left, sent_top, corner_edge, corner_side, left_rows, lay_c = call(
        upper_kernel, "upper", [phys_charge, virt, site, env, ul, top, left, sketches],
        [tall_wide, tall_wide, tagged, tagged, broad, broad, tall, lay],
        [phys_s, virt_s, keep(27, 4, 3), env_v, keep(CHI, CHI), slabs, slabs, slabs, slabs, arrivals(9),
         slabs, slabs, wide, thin, row_sum, keep(216, CHI, dtype=F32)],
        range(8),
    )
    above_range = from_behind(sent_left, "ly", 1)
    before_range = from_behind(sent_top, "lx", 1)
    from_lower, sent_lower, lower_pair = call(
        lower_kernel, "lower", [lay_b, ll, bottom, left, sketches],
        [tall_wide, tall, broad], [keep(CHI, CHI), slabs, slabs, slabs, arrivals(4), wide, thin, slabs],
        range(1, 5),
    )
    below = from_behind(sent_lower, "ly", -1)
    above, top_basis = call(
        early_kernel, "early", [from_lower, above_range, own_top, sent_top, beside],
        [tall, tall], [wide, wide],
    )
    square = keep(CUT, CUT)
    lu, le, lo, tl, te, tr = call(
        late_kernel, "late",
        [own_left, sent_left, below, from_right, before_range, above, top_basis, left_rows, rows_t,
         lay_c, lay_a, corner_edge, corner_side, lower_pair, right_pair],
        [corner, tall, corner, corner, tall, corner],
        [wide, wide, slabs, slabs, keep(CHI, CUT), keep(CHI, CUT), square, square, slabs, wide, thin, thin],
    )
    lift = lambda a: a[None, None]
    edge = lambda a: a.reshape(D2, CHI, CHI).transpose(1, 0, 2)[None, None]
    return lift(lu), edge(le), lift(lo), lift(tl), edge(te), lift(tr)


def solution(mesh):
    split = lambda rest: P("lx", "ly", *([None] * rest))
    in_specs = tuple(split(rest) for rest in (5, 1, 2, 2, 2, 2, 2, 3, 3, 3, 3, 3))
    out_specs = tuple(split(rest) for rest in (2, 3, 2, 2, 3, 2))
    return jax.shard_map(shards, mesh=mesh, in_specs=in_specs, out_specs=out_specs, check_vma=False)
```

```python
import functools

import jax
import jax.numpy as jnp
from jax import lax
from jax.experimental import pallas as pl
from jax.experimental.pallas import tpu as pltpu
from jax.sharding import PartitionSpec as P

F32 = jnp.float32
BF16 = jnp.bfloat16
CHI = 128
D2 = 9
CUT = CHI * D2
TALL = CHI * 8
LAY = 96
GROUP = 32
CHUNKS = CHI // GROUP
ROWS = GROUP * 8
VMEM = 24 * 1024 * 1024
WORK = 10_000_000


def dot(a, b):
    return lax.dot_general(a, b, (((1,), (0,)), ((), ())), preferred_element_type=F32)


def dot_nt(a, b):
    return lax.dot_general(a, b, (((1,), (1,)), ((), ())), preferred_element_type=F32)


def dot_tn(a, b):
    return lax.dot_general(a, b, (((0,), (0,)), ((), ())), preferred_element_type=F32)


def exact_tn(a, b):
    return lax.dot_general(
        a, b, (((0,), (0,)), ((), ())), precision=lax.Precision.HIGHEST, preferred_element_type=F32
    )


def exact_nt(a, b):
    return lax.dot_general(
        a, b, (((1,), (1,)), ((), ())), precision=lax.Precision.HIGHEST, preferred_element_type=F32
    )


def slab(ref, p):
    return ref[p * CHI : (p + 1) * CHI, :]


def side_by_side(ref):
    return jnp.concatenate([slab(ref, p) for p in range(D2)], axis=1)


def pack_rows(slab_of, wide, out):
    for p in range(8):
        wide[pl.ds(p, CHI, stride=8), :] = slab_of(p).astype(F32)
    out[0:TALL, :] = wide[0:TALL, :].astype(BF16)
    out[TALL:CUT, :] = slab_of(8).astype(BF16)


def packed_slab(wide, p):
    return wide[pl.ds(p, CHI, stride=8), :] if p < 8 else wide[TALL:CUT, :]


def weave(one, steps_one, two, steps_two):
    done_one = done_two = 0
    live_one = live_two = True
    while live_one or live_two:
        if live_one and (not live_two or done_one * steps_two <= done_two * steps_one):
            live_one = next(one, "end") != "end"
            done_one += 1
        else:
            live_two = next(two, "end") != "end"
            done_two += 1


def run(steps):
    for _ in steps:
        pass


CHAIN_STEPS = 3 * CHUNKS + 2


def chain(left, right, layer, thin, consume):
    thin[...] = jnp.zeros_like(thin)
    last = dot(left[TALL:CUT, :], right[...])
    for q in range(D2):
        thin[pl.ds(q, CHI, stride=16), :] = last[:, q * CHI : (q + 1) * CHI]
    yield
    blank = jnp.zeros((8, CHI), F32)

    def product(chunk):
        return dot(left[chunk * ROWS : (chunk + 1) * ROWS, :], right[...])

    def mix(chunk, three):
        stacks = []
        for f in range(GROUP):
            here = (chunk * GROUP + f) * 16
            parts = [three[f * 8 : f * 8 + 8, q * CHI : (q + 1) * CHI] for q in range(D2)]
            stack = jnp.concatenate(parts + [thin[here : here + 16, :], blank], axis=0)
            stacks.append(stack.astype(BF16))
        return dot(layer[...], jnp.concatenate(stacks, axis=1))

    def hand_on(chunk, mixed):
        tall = []
        for f in range(GROUP):
            here = (chunk * GROUP + f) * 16
            lanes = slice(f * CHI, (f + 1) * CHI)
            thin[here : here + 16, :] = mixed[72:88, lanes]
            tall.append(
                jnp.concatenate([mixed[s * 8 : s * 8 + 8, lanes] for s in range(D2)], axis=1)
            )
        rows = slice(chunk * ROWS, (chunk + 1) * ROWS)
        consume(rows, jnp.concatenate(tall, axis=0).astype(BF16))

    three = product(0)
    before = None
    for chunk in range(CHUNKS):
        following = product(chunk + 1) if chunk + 1 < CHUNKS else None
        yield
        mixed = mix(chunk, three)
        yield
        if before is not None:
            hand_on(chunk - 1, before)
        yield
        before, three = mixed, following
    hand_on(CHUNKS - 1, before)
    rest = [thin[pl.ds(s, CHI, stride=16), :].astype(BF16) for s in range(D2)]
    consume(slice(TALL, CUT), jnp.concatenate(rest, axis=1))


def third(n):
    return (n * 11) >> 5


def layer_masks():
    row = lax.broadcasted_iota(jnp.int32, (LAY, 81), 0)
    lane = lax.broadcasted_iota(jnp.int32, (LAY, 81), 1)
    late = row >= 72
    slow = jnp.where(late, row - 72, row >> 3)
    fast = jnp.where(late, 8, row & 7)
    valid = row < 81
    pairs = ((third(slow), third(fast)), (slow - 3 * third(slow), fast - 3 * third(fast)))
    leg_l = (lane * 19) >> 9
    rest = lane - 27 * leg_l
    leg_u = (rest * 57) >> 9
    rest = rest - 9 * leg_u
    leg_r = (rest * 11) >> 5
    leg_d = rest - 3 * leg_r

    def mask(slow_leg, fast_leg):
        return [
            jnp.where(valid & (slow_leg == a) & (fast_leg == b), 1.0, 0.0).astype(F32)
            for a, b in pairs
        ]

    return {
        "ru": mask(leg_r, leg_u),
        "dl": mask(leg_d, leg_l),
        "rd": mask(leg_r, leg_d),
        "ul": mask(leg_u, leg_l),
        "dr": mask(leg_d, leg_r),
        "lu": mask(leg_l, leg_u),
    }


def kept_rows(site, phys, virt, corner):
    lane = lax.broadcasted_iota(jnp.int32, (8, 81), 1)
    state = lax.broadcasted_iota(jnp.int32, (8, 81), 0)
    leg_l = (lane * 19) >> 9
    rest = lane - 27 * leg_l
    leg_u = (rest * 57) >> 9
    rest = rest - 9 * leg_u
    leg_r = (rest * 11) >> 5
    leg_d = rest - 3 * leg_r
    total = jnp.zeros((8, 81), jnp.int32)
    for s in range(4):
        total = total + jnp.where(state == s, phys[0, 0, s], 0)
    for i in range(3):
        total = total + jnp.where(leg_l == i, virt[i, 0, 0], 0)
        total = total + jnp.where(leg_u == i, virt[i, 0, 1], 0)
        total = total - jnp.where(leg_r == i, virt[i, 0, 2], 0)
        total = total - jnp.where(leg_d == i, virt[i, 0, 3], 0)
    corner[...] = jnp.zeros_like(corner)
    for n in range(27):
        corner[8 * n : 8 * n + 4, 0:3] = site[n].astype(F32)
    lane = lax.broadcasted_iota(jnp.int32, (CHI, 81), 1)
    leg = lax.broadcasted_iota(jnp.int32, (CHI, 81), 0)
    place = jnp.where(lane - 3 * ((lane * 683) >> 11) == leg, 1.0, 0.0).astype(BF16)
    wide_site = dot(corner[...].astype(BF16), place)
    block = lax.broadcasted_iota(jnp.int32, (216, 81), 0) >> 3
    lane = lax.broadcasted_iota(jnp.int32, (216, 81), 1)
    wide_site = jnp.where((lane * 683) >> 11 == block, wide_site, 0.0)
    rows = wide_site[0:8]
    for n in range(1, 27):
        rows = rows + wide_site[8 * n : 8 * n + 8]
    return jnp.where(total == 0, rows, 0.0)


def build_layers(kept, *wanted):
    masks = layer_masks()

    for out, rows, cols in wanted:
        halves_of = []
        for half in range(2):
            tall = jnp.concatenate(
                [masks[rows][half] * kept[s : s + 1, :] for s in range(4)], axis=0
            )
            halves_of.append(dot_nt(tall.astype(BF16), masks[cols][half].astype(BF16)))
        ket_bra = halves_of[0] * halves_of[1]
        total = ket_bra[:LAY]
        for s in range(1, 4):
            total = total + ket_bra[s * LAY : (s + 1) * LAY]
        out[...] = total.astype(BF16)


def unpack_term(wide, term, sent):
    for p in range(D2):
        part = packed_slab(wide, p)
        term[p * CHI : (p + 1) * CHI, :] = part
        sent[p * CHI : (p + 1) * CHI, :] = part.astype(BF16)


def add_charges(sent, env, virt, leg):
    sent[CUT : CUT + 16, :] = jnp.concatenate(
        [env]
        + [
            jnp.full((1, CHI), (virt[p // 3, 0, leg] - virt[p % 3, 0, leg]).astype(F32))
            for p in range(D2)
        ]
        + [jnp.zeros((6, CHI), F32)],
        axis=0,
    ).astype(BF16)


def bring(sources, targets, arrived):
    copies = [
        pltpu.make_async_copy(source, target, arrived.at[i])
        for i, (source, target) in enumerate(zip(sources, targets))
    ]
    for copy in copies:
        copy.start()
    return copies


def right_kernel(
    phys_h, virt_h, site_h, corner_h, edge_h, edge_rows_h, sketches,
    term, sent, pair_out, cols_out, lay_b, lay_d,
    phys, virt, site, corner, edge, edge_rows, sketch, arrived, wide, thin, small, rows_out, lay_a,
):
    copies = bring(
        (phys_h, virt_h, site_h, corner_h, edge_h, edge_rows_h, sketches.at[pl.ds(3 * CUT, CUT), :]),
        (phys, virt, site, corner, edge, edge_rows, sketch),
        arrived,
    )
    for copy in copies[:3]:
        copy.wait()
    kept = kept_rows(site, phys, virt, small)
    for copy in copies[3:]:
        copy.wait()
    build_layers(kept, (lay_a, "dl", "ru"), (lay_b, "ru", "dl"), (lay_d, "dr", "lu"))
    pack_rows(lambda p: jnp.transpose(slab(edge_rows, p).astype(F32)), wide, cols_out)
    corner_product((), corner, edge, edge_rows, sketch, lay_a, term, sent, pair_out, rows_out, wide, thin)


def lower_kernel(
    layer, corner_h, edge_h, edge_rows_h, sketches,
    term, sent, pair_out,
    corner, edge, edge_rows, sketch, arrived, wide, thin, rows_out,
):
    copies = bring(
        (corner_h, edge_h, edge_rows_h, sketches.at[pl.ds(CUT, CUT), :]),
        (corner, edge, edge_rows, sketch),
        arrived,
    )
    corner_product(copies, corner, edge, edge_rows, sketch, layer, term, sent, pair_out, rows_out, wide, thin)


def corner_product(
    copies, corner, edge, edge_rows, sketch, layer, term, sent, pair_out, rows_out, wide, thin
):
    for copy in copies[:2]:
        copy.wait()
    pair_out[...] = dot(corner[...], side_by_side(edge)).astype(BF16)
    for copy in copies[2:]:
        copy.wait()
    pack_rows(lambda p: slab(edge_rows, p), wide, rows_out)

    def consume(rows, block):
        wide[rows, :] = dot(block, sketch[...])

    run(chain(rows_out, pair_out, layer, thin, consume))
    unpack_term(wide, term, sent)


def upper_kernel(
    phys_h, virt_h, site_h, env_h, corner_h, edge_t_h, edge_l_h, sketches,
    own_left, own_top, sent_left, sent_top, corner_edge, corner_side, left_rows, lay_c,
    phys, virt, site, env, corner, edge_t, edge_l, sketch_l, sketch_t, arrived,
    sketch_cols, sketch_rows, wide, thin, top_sum, small,
):
    first = sketches.at[pl.ds(0, CUT), :]
    third_one = sketches.at[pl.ds(2 * CUT, CUT), :]
    copies = bring(
        (corner_h, edge_t_h, edge_l_h, phys_h, virt_h, site_h, env_h, first, third_one),
        (corner, edge_t, edge_l, phys, virt, site, env, sketch_l, sketch_t),
        arrived,
    )
    top_sum[...] = jnp.zeros_like(top_sum)
    for copy in copies:
        copy.wait()
    kept = kept_rows(site, phys, virt, small)
    charges = env[...].astype(F32)
    add_charges(sent_left, charges[0:1], virt, 3)
    add_charges(sent_top, charges[1:2], virt, 2)
    corner_edge[...] = dot(corner[...], side_by_side(edge_t)).astype(BF16)
    corner_side[...] = dot_tn(corner[...], side_by_side(edge_l)).astype(BF16)
    build_layers(kept, (lay_c, "rd", "ul"))
    pack_rows(lambda p: jnp.transpose(slab(edge_l, p).astype(F32)), wide, left_rows)
    wide[...] = sketch_l[...].astype(F32)
    for p in range(D2):
        sketch_cols[p * CHI : (p + 1) * CHI, :] = wide[pl.ds(p, CHI, stride=D2), :].astype(BF16)
    wide[...] = sketch_t[...].astype(F32)
    picked = [wide[pl.ds(p, CHI, stride=D2), :] for p in range(D2)]
    pack_rows(lambda p: picked[p], wide, sketch_rows)

    def consume(rows, block):
        wide[rows, :] = dot(block, sketch_cols[...])
        top_sum[...] += dot_tn(sketch_rows[rows, :], block)

    run(chain(left_rows, corner_edge, lay_c, thin, consume))
    unpack_term(wide, own_left, sent_left)
    for p in range(D2):
        part = jnp.transpose(top_sum[:, p * CHI : (p + 1) * CHI])
        own_top[p * CHI : (p + 1) * CHI, :] = part
        sent_top[p * CHI : (p + 1) * CHI, :] = part.astype(BF16)


BLOCK = 32


def reciprocal(x):
    r = pl.reciprocal(x, approx=True)
    return r * (2.0 - x * r)


def spread(rows, p):
    return jnp.broadcast_to(rows[p : p + 1, :], (8, CHI))


STEPS = CHI // 2


def eliminate(grams, result):
    count = len(grams)
    sub = lax.broadcasted_iota(jnp.int32, (8, CHI), 0)
    lane = lax.broadcasted_iota(jnp.int32, (8, CHI), 1)
    groups = CHI // 8
    fact = [[g[8 * i : 8 * i + 8, :] for i in range(groups)] for g in grams]
    inv = [
        [jnp.where(lane == sub + 8 * i, 1.0, 0.0).astype(F32) for i in range(groups)] for _ in grams
    ]
    for start in range(0, groups, BLOCK // 8):
        end = start + BLOCK // 8
        for b in range(start, end):
            cols = [
                [
                    [
                        jnp.broadcast_to(fact[m][g][:, 8 * b + j : 8 * b + j + 1], (8, CHI))
                        for j in range(8)
                    ]
                    for g in range(b, end)
                ]
                for m in range(count)
            ]
            pivots = [jnp.zeros((8, CHI), F32) for _ in grams]
            for p in range(0, 8, 2):
                q = p + 1
                for m in range(count):
                    head = cols[m][0]
                    one, off, two = spread(head[p], p), spread(head[q], p), spread(head[q], q)
                    det = one * two - off * off
                    over_one, over_det = reciprocal(one), reciprocal(det)
                    lead = off * over_one
                    pivots[m] = jnp.where(
                        sub == p, one, jnp.where(sub == q, det * over_one, pivots[m])
                    )
                    later = range(q + 1, 8)
                    row_p = [spread(head[j], p) for j in later]
                    row_q = [spread(head[j], q) for j in later]
                    fact_p, fact_q = spread(fact[m][b], p), spread(fact[m][b], q)
                    inv_p, inv_q = spread(inv[m][b], p), spread(inv[m][b], q)
                    one_d, off_d, two_d = one * over_det, off * over_det, two * over_det
                    for g in range(b, end):
                        own = cols[m][g - b]
                        by_p = own[p] * two_d - own[q] * off_d
                        by_q = own[q] * one_d - own[p] * off_d
                        if g == b:
                            by_p = jnp.where(sub > q, by_p, jnp.where(sub == q, lead, 0.0))
                            by_q = jnp.where(sub > q, by_q, 0.0)
                        for n, j in enumerate(later):
                            own[j] = own[j] - by_p * row_p[n] - by_q * row_q[n]
                        fact[m][g] = fact[m][g] - by_p * fact_p - by_q * fact_q
                        inv[m][g] = inv[m][g] - by_p * inv_p - by_q * inv_q
                yield
            for m in range(count):
                root = lax.rsqrt(pivots[m])
                fact[m][b] = fact[m][b] * root
                inv[m][b] = inv[m][b] * root
        if end < groups:
            for m in range(count):
                upper = jnp.concatenate(fact[m][start:end], axis=0)
                both = jnp.concatenate([upper, jnp.concatenate(inv[m][start:end], axis=0)], axis=1)
                update = exact_tn(upper, both)
                for g in range(end, groups):
                    fact[m][g] = fact[m][g] - update[8 * g : 8 * g + 8, :CHI]
                    inv[m][g] = inv[m][g] - update[8 * g : 8 * g + 8, CHI:]
    result.extend(jnp.concatenate(i, axis=0) for i in inv)


def halves(values):
    high = values.astype(BF16)
    return high, (values - high.astype(F32)).astype(BF16)


def gram_of(ranged):
    high, low = halves(ranged)
    both = dot_tn(high, jnp.concatenate([high, low], axis=1))
    cross = both[:, CHI:]
    return both[:, :CHI] + (cross + jnp.transpose(cross))


def times_inverse(ranged, inverse):
    high, low = halves(ranged)
    inv_high, inv_low = halves(inverse)
    factors = jnp.concatenate(
        [
            jnp.concatenate([inv_high, inv_high], axis=1),
            jnp.concatenate([inv_low, jnp.zeros_like(inv_low)], axis=1),
        ],
        axis=0,
    )
    both = dot_nt(jnp.concatenate([high, low], axis=1), factors)
    return both[:, :CHI] + both[:, CHI:]


def unit(values):
    square = jnp.sum(jnp.sum(values * values, axis=1, keepdims=True), axis=0, keepdims=True)
    return (values / jnp.sqrt(square / values.size + 1e-06)).astype(BF16)


def slab_rows(wide_ref, p):
    return wide_ref[:, p * CHI : (p + 1) * CHI]


def corner_from(projector, pair):
    tall = jnp.concatenate([slab_rows(pair, p) for p in range(D2)], axis=0)
    return dot_tn(projector[...], tall)


def range_and_gram(own, other, tagged, ranged):
    row = lax.broadcasted_iota(jnp.int32, (CHI, CHI), 0)
    col = lax.broadcasted_iota(jnp.int32, (CHI, CHI), 1)
    tags = tagged[CUT : CUT + 16, :].astype(F32)
    across = jnp.broadcast_to(tags[0:1], (CHI, CHI))
    gap = across - jnp.transpose(across)
    for p in range(D2):
        sums = slab(own, p) + slab(other, p).astype(F32)
        ranged[p * CHI : (p + 1) * CHI, :] = jnp.where(gap == tags[1 + p : 2 + p], sums, 0.0)
    gram = gram_of(ranged[...])
    diagonal = jnp.where(row == col, gram, 0.0)
    mean = jnp.sum(jnp.sum(diagonal, axis=1, keepdims=True), axis=0, keepdims=True) / CHI
    return gram + jnp.where(row == col, 0.01 * mean + 1e-06, 0.0)


def early_kernel(
    from_lower, above_range, from_right, before_range,
    above, before,
    range_a, range_b,
):
    grams = [
        range_and_gram(from_lower, above_range, above_range, range_a),
        range_and_gram(from_right, before_range, before_range, range_b),
    ]
    inverses = []
    run(eliminate(grams, inverses))
    above[...] = times_inverse(range_a[...], inverses[0]).astype(BF16)
    before[...] = times_inverse(range_b[...], inverses[1]).astype(BF16)


def late_kernel(
    own_left, sent_left, below, own_top, sent_top, beside, above, before,
    left_rows, top_cols, lay_c, lay_d, corner_edge, corner_side, lower_pair, right_pair,
    out_lu, out_le, out_ll, out_tl, out_te, out_tr,
    range_l, range_t, left, top, beside_a, beside_b, mixed_l, mixed_t, packed, wide, thin_l, thin_t,
):
    grams = [
        range_and_gram(own_left, below, sent_left, range_l),
        range_and_gram(own_top, beside, sent_top, range_t),
    ]

    def keep_l(rows, block):
        mixed_l[rows, :] = block

    def keep_t(rows, block):
        mixed_t[rows, :] = block

    def products():
        beside_b[...] = side_by_side(before)
        yield from chain(top_cols, beside_b, lay_d, thin_t, keep_t)
        beside_a[...] = side_by_side(above)
        yield from chain(left_rows, beside_a, lay_c, thin_l, keep_l)
        out_lu[...] = unit(corner_from(above, corner_edge))
        out_tl[...] = unit(jnp.transpose(corner_from(before, corner_side)))

    inverses = []
    weave(eliminate(grams, inverses), STEPS, products(), 2 * CHAIN_STEPS)
    left[...] = times_inverse(range_l[...], inverses[0]).astype(BF16)
    top[...] = times_inverse(range_t[...], inverses[1]).astype(BF16)
    out_ll[...] = unit(corner_from(left, lower_pair))
    out_tr[...] = unit(corner_from(top, right_pair))
    for basis, mixed, out in ((left, mixed_l, out_le), (top, mixed_t, out_te)):
        pack_rows(lambda p: slab(basis, p), wide, packed)
        result = unit(dot_tn(packed[...], mixed[...]))
        for p in range(D2):
            part = result[:, p * CHI : (p + 1) * CHI]
            out[p * CHI : (p + 1) * CHI, :] = jnp.transpose(part)


def shape(*dims, dtype=BF16):
    return jax.ShapeDtypeStruct(dims, dtype)


def call(body, name, ins, outs, scratch, far=()):
    moved = sum(a.size * a.dtype.itemsize for a in ins) + sum(
        o.size * jnp.dtype(o.dtype).itemsize for o in outs
    )
    whole = pl.BlockSpec(memory_space=pltpu.VMEM)
    return pl.pallas_call(
        body,
        name=name,
        out_shape=tuple(outs),
        in_specs=[
            pl.BlockSpec(memory_space=pltpu.HBM) if i in far else whole for i in range(len(ins))
        ],
        out_specs=(whole,) * len(outs),
        scratch_shapes=scratch,
        compiler_params=pltpu.CompilerParams(vmem_limit_bytes=VMEM if name != "upper" else 60 * 1024 * 1024),
        cost_estimate=pl.CostEstimate(flops=1, bytes_accessed=1, transcendentals=0),
    )(*ins)


def from_behind(block, axis, distance):
    size = lax.axis_size(axis)
    route = [((i - distance) % size, i) for i in range(size)]
    return lax.ppermute(block, axis, route)


def flat(edge):
    return edge.transpose(1, 0, 2).reshape(CUT, CHI)


def shards(
    site_tensor, phys_charge, virt_charge, env_charge, corner_ul, corner_ur, corner_ll,
    edge_top, edge_right, edge_bottom, edge_left, sketch,
):
    site = site_tensor.transpose(0, 1, 3, 4, 5, 2, 6).reshape(27, 4, 3)
    virt = virt_charge.transpose(0, 3, 1, 2).reshape(3, 1, 4)
    env = env_charge[0, 0]
    ul, ur, ll = corner_ul[0, 0], corner_ur[0, 0], corner_ll[0, 0]
    top, right, bottom, left = (
        flat(e[0, 0]) for e in (edge_top, edge_right, edge_bottom, edge_left)
    )
    sketches = sketch[0, 0].reshape(4 * CUT, CHI)
    tall = shape(CUT, CHI)
    tall_wide = shape(CUT, CHI, dtype=F32)
    tagged = shape(CUT + 16, CHI)
    broad = shape(CHI, CUT)
    lay = shape(LAY, LAY)
    corner = shape(CHI, CHI)
    keep = lambda *dims, dtype=BF16: pltpu.VMEM(dims, dtype)
    slabs = keep(CUT, CHI)
    wide = keep(CUT, CHI, dtype=F32)
    thin = keep(CHI * 16, CHI, dtype=F32)
    row_sum = keep(CHI, CUT, dtype=F32)
    phys_s = pltpu.SMEM((1, 1, 4), jnp.int32)
    virt_s = pltpu.SMEM((3, 1, 4), jnp.int32)
    env_v = keep(2, CHI, dtype=jnp.int32)
    arrivals = lambda n: pltpu.SemaphoreType.DMA((n,))
    from_right, sent_right, right_pair, top_cols, lay_b, lay_d = call(
        right_kernel, "right", [phys_charge, virt, site, ur, right, top, sketches],
        [tall_wide, tall, broad, tall, lay, lay],
        [phys_s, virt_s, keep(27, 4, 3), keep(CHI, CHI), slabs, slabs, slabs, arrivals(7), wide, thin,
         keep(216, CHI, dtype=F32), slabs, keep(LAY, LAY)],
        range(7),
    )
    beside = from_behind(sent_right, "lx", -1)
    own_left, own_top, sent_left, sent_top, corner_edge, corner_side, left_rows, lay_c = call(
        upper_kernel, "upper", [phys_charge, virt, site, env, ul, top, left, sketches],
        [tall_wide, tall_wide, tagged, tagged, broad, broad, tall, lay],
        [phys_s, virt_s, keep(27, 4, 3), env_v, keep(CHI, CHI), slabs, slabs, slabs, slabs, arrivals(9),
         slabs, slabs, wide, thin, row_sum, keep(216, CHI, dtype=F32)],
        range(8),
    )
    above_range = from_behind(sent_left, "ly", 1)
    before_range = from_behind(sent_top, "lx", 1)
    from_lower, sent_lower, lower_pair = call(
        lower_kernel, "lower", [lay_b, ll, bottom, left, sketches],
        [tall_wide, tall, broad], [keep(CHI, CHI), slabs, slabs, slabs, arrivals(4), wide, thin, slabs],
        range(1, 5),
    )
    below = from_behind(sent_lower, "ly", -1)
    above, before = call(
        early_kernel, "early", [from_lower, above_range, from_right, before_range],
        [tall, tall], [wide, wide],
    )
    square = keep(CUT, CUT)
    lu, le, lo, tl, te, tr = call(
        late_kernel, "late",
        [own_left, sent_left, below, own_top, sent_top, beside, above, before, left_rows, top_cols,
         lay_c, lay_d, corner_edge, corner_side, lower_pair, right_pair],
        [corner, tall, corner, corner, tall, corner],
        [wide, wide, slabs, slabs, keep(CHI, CUT), keep(CHI, CUT), square, square, slabs, wide, thin, thin],
    )
    lift = lambda a: a[None, None]
    edge = lambda a: a.reshape(D2, CHI, CHI).transpose(1, 0, 2)[None, None]
    return lift(lu), edge(le), lift(lo), lift(tl), edge(te), lift(tr)


def solution(mesh):
    split = lambda rest: P("lx", "ly", *([None] * rest))
    in_specs = tuple(split(rest) for rest in (5, 1, 2, 2, 2, 2, 2, 3, 3, 3, 3, 3))
    out_specs = tuple(split(rest) for rest in (2, 3, 2, 2, 3, 2))
    return jax.shard_map(shards, mesh=mesh, in_specs=in_specs, out_specs=out_specs, check_vma=False)
```
